128 devices in a mesh: row: 16 (over y, z), col: 8 (over x, core).
Axes of the slice: x: 4, y: 4, z: 4, core: 2. Of those that a mesh axis runs over, the one named last changes fastest.
Arguments:
- panel: float32 [196608, 1024], P('row', 'col'), may hold values from -6 to 6
- test_matrix: float32 [1024, 128], P('col'), may hold values from -0.1875 to 0.1875
- prior_sketch: float32 [196608, 128], P(('row', 'col')), may hold values from -180 to 180, as said below
Outputs:
- basis: float32 [196608, 128], P(('row', 'col'))
- projected: float32 [128, 1024], P('row', 'col')
The draws below stay inside these ranges and needn't reach their ends.
Inputs may be any that keep to these rules, and one draw needn't show every extreme that they name: `prior_sketch`: real entries of full rank; columns differ in scale.
All inputs are finite; a program needn't handle non-finite values.
Results may differ from the reference program's by a relative error of at most 0.0003.
Values sent between devices are 32-bit elements; how exact they have to be, the bound alone decides.
No kernel may reach another device: no remote copies, remote signals or barrier semaphores. Data moves between devices by JAX's collectives and lax.ppermute only.
A program may use at most 128 MiB of HBM per device.

```python
import jax
import jax.numpy as jnp
from jax import lax

RANK = 128
PANEL = 1024
ROWS = 196608


def draw_prior_sketch(key, part):
    key = jax.random.fold_in(key, 1)
    first, second = jax.random.split(key, 2)
    col_scale = jnp.exp(jax.random.uniform(second, (RANK,), jnp.float32, 0.0, 2.302585))
    row_scale = 1.0 + 2.0 * jnp.arange(ROWS, dtype=jnp.float32) / ROWS
    base = jax.random.normal(first, (ROWS, RANK), jnp.float32)
    base = jnp.clip(base, -6.0, 6.0)
    return base * row_scale[:, None] * col_scale[None, :]


def block_levels(own_key, shape, pieces, smallest, high):
    level, own = 1.0, jax.random.fold_in(own_key, 6)
    for dim, parts in pieces:
        heights = jnp.exp(jax.random.uniform(jax.random.fold_in(own, dim), (parts,), jnp.float32, smallest / len(pieces), high / len(pieces)))
        level = level * jnp.repeat(heights, shape[dim] // parts).reshape([-1 if axis == dim else 1 for axis in range(len(shape))])
    return level


def centred(own_key, extent, scale, bound, cuts=(), kind=jnp.bfloat16):
    values = scale * jax.random.normal(own_key, extent, jnp.float32)
    if cuts:
        values = values * block_levels(own_key, extent, cuts, -0.22, 0.18)
    return jnp.clip(values, -bound, bound).astype(kind)


def setup_inputs(seed: int = 0) -> dict:
    key_of = jax.random.split(jax.random.key(seed), 4)
    panel = centred(key_of[0], (ROWS, PANEL), 1.0, 6.0, ((0, 16), (1, 8)), jnp.float32)
    test_matrix = centred(key_of[1], (PANEL, RANK), PANEL ** -0.5, 0.1875, ((0, 8),), jnp.float32)
    prior_sketch = draw_prior_sketch(jax.random.fold_in(key_of[3], 71), 0)
    return {"panel": panel, "test_matrix": test_matrix, "prior_sketch": prior_sketch}


def reference(panel, test_matrix, prior_sketch):
    sketch = prior_sketch + jnp.dot(panel.astype(jnp.float32), test_matrix.astype(jnp.float32), precision=lax.Precision.HIGHEST, preferred_element_type=jnp.float32)
    orthonormal, upper = jnp.linalg.qr(sketch)
    signs = jnp.sign(jnp.diagonal(upper))
    orthonormal = orthonormal * signs[None, :]
    basis = orthonormal * jnp.sqrt(jnp.float32(ROWS))
    projected = jnp.dot(orthonormal.T.astype(jnp.float32), panel.astype(jnp.float32), precision=lax.Precision.HIGHEST, preferred_element_type=jnp.float32)
    return (basis, projected)
```

```python
import jax
import jax.numpy as jnp
from jax import lax
from jax.sharding import Mesh, PartitionSpec as P

HIGH = lax.Precision.HIGH
HIGHEST = lax.Precision.HIGHEST
AXES = ("y", "z", "x", "core")


def shift(block, axis, by):
    n = lax.axis_size(axis)
    return lax.ppermute(block, axis, [(i, (i + by) % n) for i in range(n)])


def swap(block):
    return shift(block, "core", 1)


def axis_sum(block, axis):
    near = block + shift(block, axis, 1)
    return near + shift(near, axis, 2)


def axis_scatter(block, axis):
    me = lax.axis_index(axis)
    n = lax.axis_size(axis)
    parts = block.reshape((n, block.shape[0] // n) + block.shape[1:])
    take = lambda i: lax.dynamic_index_in_dim(parts, (me + i) % n, 0, keepdims=False)
    total = take(0)
    for by in (2, 1, 3):
        total = total + shift(take(by), axis, by)
    return total


def dot(a, b, precision=HIGH):
    return jnp.dot(a, b, precision=precision, preferred_element_type=jnp.float32)


def shards(panel, test_matrix, prior_sketch):
    x = lax.axis_index("x")
    core = lax.axis_index("core")
    rows = prior_sketch.shape[0]
    half = rows // 2
    rank = prior_sketch.shape[1]
    cols = panel.shape[1]
    total_rows = panel.shape[0] * lax.axis_size("y") * lax.axis_size("z")

    blocks = panel.reshape(4, 2, rows, cols)
    pick = lambda d, c: lax.dynamic_slice(blocks, (d, c, 0, 0), (1, 1, rows, cols))[0, 0]
    test_other = swap(test_matrix)
    mine, other, part = [], [], []
    for step in (2, 1, 3, 0):
        d = (x + step) % 4
        mine.append(pick(d, core))
        other.append(swap(pick(d, 1 - core)))
        part.append(dot(mine[-1], test_matrix) + dot(other[-1], test_other))
    far, right, left, here = part

    far_top = shift(far[:half], "x", 1)
    far_bot = shift(far[half:], "x", 3)
    near_bot = shift(right[half:], "x", 1)
    near_top = shift(left[:half], "x", 3)
    both_top = shift(right[:half] + far_top, "x", 1)
    both_bot = shift(left[half:] + far_bot, "x", 3)
    base = here + prior_sketch
    own_top = base[:half] + near_top + both_top
    own_bot = base[half:] + near_bot + both_bot

    from_left_bot = shift(own_bot, "x", 1)
    from_right_top = shift(own_top, "x", 3)
    from_left_top = shift(own_top, "x", 1)
    from_right_bot = shift(own_bot, "x", 3)
    from_far_bot = shift(from_left_bot, "x", 1)
    from_far_top = shift(from_right_top, "x", 3)

    own = jnp.concatenate([own_top, own_bot], 0)
    gram = dot(own.T, own, HIGHEST)
    for axis in ("y", "z", "x"):
        gram = axis_sum(gram, axis)
    gram = gram + swap(gram)
    lower = jnp.linalg.cholesky(gram)
    inverse = lax.linalg.triangular_solve(
        lower, jnp.eye(rank, dtype=jnp.float32), left_side=True, lower=True
    )
    scale = jnp.sqrt(jnp.float32(total_rows))
    basis = dot(own, inverse.T * scale, HIGHEST)

    tops = (from_far_top, from_right_top, from_left_top, own_top)
    bots = (from_far_bot, from_right_bot, from_left_bot, own_bot)
    keep = jnp.zeros((rank, cols), jnp.float32)
    give = jnp.zeros((rank, cols), jnp.float32)
    for order in (3, 1, 2, 0):
        for rows_in, span in ((tops, slice(0, half)), (bots, slice(half, rows))):
            keep = keep + dot(rows_in[order].T, mine[order][span])
            give = give + dot(rows_in[order].T, other[order][span])
    weights = dot(inverse, keep + swap(give), HIGHEST)
    projected = axis_scatter(axis_scatter(weights, "y"), "z")
    return basis, projected


def solution(mesh):
    fine = Mesh(mesh.devices.reshape(4, 4, 4, 2), AXES)
    return jax.shard_map(
        shards,
        mesh=fine,
        in_specs=(P(("y", "z"), ("x", "core")), P(("x", "core"), None), P(AXES, None)),
        out_specs=(P(AXES, None), P(("y", "z"), ("x", "core"))),
        check_vma=False,
    )
```

```python
import functools

import jax
import jax.numpy as jnp
from jax import lax
from jax.experimental import pallas as pl
from jax.experimental.pallas import tpu as pltpu
from jax.sharding import Mesh, PartitionSpec as P

AXES = ("y", "z", "x", "core")
F32 = jnp.float32
BF16 = jnp.bfloat16
LIMIT = 16 * 1024 * 1024
COST = pl.CostEstimate(flops=0, bytes_accessed=0, transcendentals=0)
PARAMS = pltpu.CompilerParams(vmem_limit_bytes=LIMIT)
WHOLE = pl.BlockSpec(memory_space=pltpu.VMEM)
SCALAR = pl.BlockSpec(memory_space=pltpu.SMEM)


def shift(block, axis, by):
    n = lax.axis_size(axis)
    return lax.ppermute(block, axis, [(i, (i + by) % n) for i in range(n)])


def swap(block):
    return shift(block, "core", 1)


def trade(block, axis, stage):
    partner = (3, 2, 1, 0) if stage == 0 else (1, 0, 3, 2)
    return lax.ppermute(block, axis, [(i, partner[i]) for i in range(4)])


def axis_sum(block, axis):
    for stage in (0, 1):
        block = block + trade(block, axis, stage)
    return block


def axis_scatter(block, axis):
    me = lax.axis_index(axis)
    for stage, upper in ((0, me // 2), (1, me % 2)):
        half = block.shape[0] // 2
        keep = lax.dynamic_slice_in_dim(block, upper * half, half, 0)
        give = lax.dynamic_slice_in_dim(block, (1 - upper) * half, half, 0)
        block = keep + trade(give, axis, stage)
    return block


def split(block):
    high = block.astype(BF16)
    return high, (block - high.astype(F32)).astype(BF16)


def mm(a, b):
    return jnp.dot(a, b, preferred_element_type=F32)


def fetch_body(place_ref, panel_ref, *rest, count):
    outs, sems = rest[:count], rest[count]
    rows = outs[0].shape[0]
    copies = []
    for slot, out_ref in enumerate(outs):
        start = pl.multiple_of(place_ref[slot] * rows, rows)
        copies.append(
            pltpu.make_async_copy(panel_ref.at[pl.ds(start, rows), :], out_ref, sems.at[slot])
        )
    for copy in copies:
        copy.start()
    for copy in copies:
        copy.wait()


def fetch(places, panel, rows):
    count = places.shape[0]
    cols = panel.shape[1]
    return pl.pallas_call(
        functools.partial(fetch_body, count=count),
        out_shape=[pltpu.VMEM((rows, cols), F32)] * count,
        in_specs=[SCALAR, pl.BlockSpec(memory_space=pl.ANY)],
        out_specs=[WHOLE] * count,
        scratch_shapes=[pltpu.SemaphoreType.DMA((count,))],
        compiler_params=PARAMS,
        cost_estimate=COST,
        name="fetch",
    )(places, panel)


def term_body(mine_ref, other_ref, test_ref, test_other_ref, *rest, first, spans, block):
    rank = test_ref.shape[1]
    tests = jnp.concatenate([test_ref[...], test_other_ref[...]], 0)
    tests = jnp.concatenate(split(tests), 1)
    out_ref = rest[-1]
    for at in range(0, out_ref.shape[0], block):
        here = slice(first + at, first + at + block)
        high, low = split(jnp.concatenate([mine_ref[here, :], other_ref[here, :]], 1))
        both = mm(low, tests) + mm(high, tests)
        total = both[:, rank:] + both[:, :rank]
        for addend_ref, start in zip(rest[:-1], spans):
            total = total + addend_ref[start + at : start + at + block, :]
        out_ref[at : at + block, :] = total


def term(chunk, first, count, tests, *addends, block=384):
    rank = tests[0].shape[1]
    return pl.pallas_call(
        functools.partial(
            term_body, first=first, spans=[0 for _ in addends], block=block
        ),
        out_shape=pltpu.VMEM((count, rank), F32),
        in_specs=[WHOLE] * (4 + len(addends)),
        out_specs=WHOLE,
        compiler_params=PARAMS,
        cost_estimate=COST,
        name="term",
    )(*chunk, *tests, *addends)


def finish_body(base_ref, near_top_ref, near_bot_ref, both_top_ref, both_bot_ref, own_ref, turned_ref):
    half = near_top_ref.shape[0]
    for part, near_ref, both_ref in ((0, near_top_ref, both_top_ref), (1, near_bot_ref, both_bot_ref)):
        span = slice(part * half, (part + 1) * half)
        own = base_ref[span, :] + near_ref[...] + both_ref[...]
        own_ref[span, :] = own
        turned_ref[part] = own.T


def finish(base, *others):
    rows, rank = base.shape
    return pl.pallas_call(
        finish_body,
        out_shape=(
            pltpu.VMEM((rows, rank), F32),
            pltpu.VMEM((2, rank, rows // 2), F32),
        ),
        in_specs=[WHOLE] * 5,
        out_specs=(WHOLE, WHOLE),
        compiler_params=PARAMS,
        cost_estimate=COST,
        name="finish",
    )(base, *others)


def gram_body(core_ref, own_ref, turned_ref, keep_ref, give_ref, work_ref):
    half = keep_ref.shape[0]
    rows = turned_ref.shape[2]
    dot = functools.partial(jnp.dot, precision=lax.Precision.HIGHEST, preferred_element_type=F32)
    work_ref[...] = dot(turned_ref[0], own_ref[:rows, :]) + dot(turned_ref[1], own_ref[rows:, :])
    core = core_ref[0]
    keep_ref[...] = work_ref[pl.ds(pl.multiple_of(core * half, half), half), :]
    give_ref[...] = work_ref[pl.ds(pl.multiple_of((1 - core) * half, half), half), :]


def gram_of(core, own, turned):
    rank = own.shape[1]
    out = jax.ShapeDtypeStruct((rank // 2, rank), F32)
    return pl.pallas_call(
        gram_body,
        out_shape=(out, out),
        in_specs=[SCALAR] + [WHOLE] * 2,
        out_specs=(WHOLE, WHOLE),
        scratch_shapes=[pltpu.VMEM((rank, rank), F32)],
        compiler_params=PARAMS,
        cost_estimate=COST,
        name="gram",
    )(core, own, turned)


def factor_body(core_ref, mine_ref, other_ref, inverse_ref, turned_ref, *, scale, tile=8):
    half, n = mine_ref.shape
    blocks = n // tile
    first = core_ref[0] == 0
    upper = jnp.where(first, mine_ref[...], other_ref[...])
    lower = jnp.where(first, other_ref[...], mine_ref[...])
    gram = jnp.concatenate([upper, lower], 0)
    row = lax.broadcasted_iota(jnp.int32, (tile, n), 0)
    lane = lax.broadcasted_iota(jnp.int32, (tile, n), 1)
    mat = [gram[tile * r : tile * (r + 1), :] for r in range(blocks)]
    out = [jnp.where(lane == row + tile * r, 1.0, 0.0).astype(F32) for r in range(blocks)]
    for b in range(blocks):
        live = range(b, blocks)
        col = [
            {r: jnp.broadcast_to(mat[r][:, tile * b + s : tile * b + s + 1], (tile, n)) for r in live}
            for s in range(tile)
        ]
        inv = []
        for s in range(tile):
            inv.append(lax.rsqrt(col[s][b][s : s + 1, :]))
            for r in live:
                col[s][r] = col[s][r] * inv[s]
            for t in range(s + 1, tile):
                factor = col[s][b][t : t + 1, :]
                for r in live:
                    col[t][r] = col[t][r] - col[s][r] * factor
        top, left = mat[b], out[b]
        tops, lefts = [], []
        for s in range(tile):
            tops.append(top[s : s + 1, :] * inv[s])
            lefts.append(left[s : s + 1, :] * inv[s])
            if s + 1 < tile:
                low = jnp.where(row > s, col[s][b], 0.0)
                top = top - low * tops[s]
                left = left - low * lefts[s]
        inverse_ref[tile * b : tile * (b + 1), :] = jnp.concatenate(lefts, 0)
        for r in range(b + 1, blocks):
            for s in range(tile):
                mat[r] = mat[r] - col[s][r] * tops[s]
                out[r] = out[r] - col[s][r] * lefts[s]
    turned_ref[...] = inverse_ref[...].T * scale


def factor_inverse(core, mine, other, scale):
    rank = mine.shape[1]
    out = jax.ShapeDtypeStruct((rank, rank), F32)
    return pl.pallas_call(
        functools.partial(factor_body, scale=scale),
        out_shape=(out, out),
        in_specs=[SCALAR, WHOLE, WHOLE],
        out_specs=(WHOLE, WHOLE),
        compiler_params=PARAMS,
        cost_estimate=COST,
        name="factor",
    )(core, mine, other)


def basis_body(own_ref, turned_ref, basis_ref):
    basis_ref[...] = jnp.dot(
        own_ref[...], turned_ref[...], precision=lax.Precision.HIGHEST, preferred_element_type=F32
    )


def basis_of(own, turned):
    rows, rank = own.shape
    block = rows // 4
    return pl.pallas_call(
        basis_body,
        out_shape=jax.ShapeDtypeStruct((rows, rank), F32),
        grid=(rows // block,),
        in_specs=[
            pl.BlockSpec((block, rank), lambda i: (i, 0)),
            pl.BlockSpec((rank, rank), lambda i: (0, 0)),
        ],
        out_specs=pl.BlockSpec((block, rank), lambda i: (i, 0)),
        compiler_params=PARAMS,
        cost_estimate=COST,
        name="basis",
    )(own, turned)


def weigh_body(*refs, plan, block):
    keep_ref, give_ref = refs[-2:]
    rank, cols = keep_ref.shape
    total = None
    for turned, part, chunk, chunk_part in plan:
        size = refs[turned].shape[2]
        for at in range(0, size, block):
            rows = jnp.concatenate(split(refs[turned][part, :, at : at + block]), 0)
            here = slice(chunk_part * size + at, chunk_part * size + at + block)
            high, low = split(jnp.concatenate([refs[chunk][here, :], refs[chunk + 1][here, :]], 1))
            both = mm(rows, low) + mm(rows, high)
            total = both if total is None else total + both
    total = total[rank:] + total[:rank]
    keep, give = total[:, :cols], total[:, cols:]
    if len(refs) > 2 + max(step[2] for step in plan) + 2:
        keep = refs[-4][...] + keep
        give = refs[-3][...] + give
    keep_ref[...] = keep
    give_ref[...] = give


def weigh(turned, chunks, plan, acc=(), block=384):
    rank = turned[0].shape[1]
    cols = chunks[0][0].shape[1]
    args = list(turned) + [array for chunk in chunks for array in chunk] + list(acc)
    plan = [(t, part, len(turned) + 2 * c, chunk_part) for t, part, c, chunk_part in plan]
    return pl.pallas_call(
        functools.partial(weigh_body, plan=plan, block=block),
        out_shape=(pltpu.VMEM((rank, cols), F32),) * 2,
        in_specs=[WHOLE] * len(args),
        out_specs=(WHOLE, WHOLE),
        compiler_params=PARAMS,
        cost_estimate=COST,
        name="weigh",
    )(*args)


def project_body(core_ref, inverse_ref, keep_ref, give_ref, out_ref):
    dot = functools.partial(jnp.dot, precision=lax.Precision.HIGHEST, preferred_element_type=F32)
    rank, cols = keep_ref.shape
    keep = dot(inverse_ref[...], keep_ref[...])
    give = dot(inverse_ref[...], give_ref[...])
    first = core_ref[0] == 0
    both = jnp.concatenate([jnp.where(first, keep, give), jnp.where(first, give, keep)], 1)
    for part in range(16):
        span = slice(part * (rank // 16), (part + 1) * (rank // 16))
        out_ref[part, 0] = both[span, :cols]
        out_ref[part, 1] = both[span, cols:]


def project(core, inverse, keep, give):
    rank, cols = keep.shape
    out = pl.pallas_call(
        project_body,
        out_shape=jax.ShapeDtypeStruct((16, 2, rank // 16, cols), F32),
        in_specs=[SCALAR] + [WHOLE] * 3,
        out_specs=WHOLE,
        compiler_params=PARAMS,
        cost_estimate=COST,
        name="project",
    )(core, inverse, keep, give)
    return out.reshape(2 * rank, cols)


def shards(panel, test_matrix, prior_sketch):
    x = lax.axis_index("x")
    core = lax.axis_index("core")
    core_of = core.reshape(1)
    rows, rank = prior_sketch.shape
    half = rows // 2
    total_rows = panel.shape[0] * lax.axis_size("y") * lax.axis_size("z")

    def places(*steps):
        first = [(x + step) % 4 * 2 for step in steps]
        first = jnp.stack(first)
        return first + core, first + 1 - core

    panel = pltpu.with_memory_space_constraint(panel, pltpu.HBM)
    test_other = swap(test_matrix)
    tests = (test_matrix, test_other)
    keep, give = places(2, 1, 3, 0)
    far_give, = fetch(give[:1], panel, rows)
    panel, far_give = lax.optimization_barrier((panel, far_give))
    far_other = swap(far_give)
    far_keep, *near = fetch(jnp.concatenate([keep[:3], give[1:3]]), panel, rows)
    far = (far_keep, far_other)
    right = (near[0], swap(near[2]))
    left = (near[1], swap(near[3]))

    far_top = term(far, 0, half, tests)
    far_bot = term(far, half, half, tests)
    far_top, far_bot, right, left = lax.optimization_barrier((far_top, far_bot, right, left))
    far_top = shift(far_top, "x", 1)
    far_bot = shift(far_bot, "x", 3)
    near_bot = term(right, half, half, tests)
    near_top = term(left, 0, half, tests)
    panel, near_bot, near_top = lax.optimization_barrier((panel, near_bot, near_top))
    near_bot = shift(near_bot, "x", 1)
    near_top = shift(near_top, "x", 3)
    here_keep, here_give = fetch(jnp.stack([keep[3], give[3]]), panel, rows)
    here = (here_keep, swap(here_give))
    base = term(here, 0, rows, tests, prior_sketch)
    both_top = shift(term(right, 0, half, tests, far_top), "x", 1)
    both_bot = shift(term(left, half, half, tests, far_bot), "x", 3)
    own, turned = finish(base, near_top, near_bot, both_top, both_bot)

    from_left = shift(turned, "x", 1)
    from_right = shift(turned, "x", 3)

    keep, give = gram_of(core_of, own, turned)
    gram = keep + swap(give)
    gram = axis_sum(axis_sum(gram, "y"), "z")
    gram, turned = lax.optimization_barrier((gram, turned))
    acc = weigh([turned], [here], [(0, 0, 0, 0), (0, 1, 0, 1)])
    across = [shift(gram, "x", by) for by in (2, 1, 3)]

    acc, from_left, from_right = lax.optimization_barrier((acc, from_left, from_right))
    far_bot = shift(from_left[1:], "x", 1)
    far_top = shift(from_right[:1], "x", 3)
    acc = weigh(
        [from_left, from_right],
        [left, right],
        [(0, 0, 0, 0), (0, 1, 0, 1), (1, 0, 1, 0), (1, 1, 1, 1)],
        acc,
    )
    gram = gram + across[0] + across[1] + across[2]
    gram, acc = lax.optimization_barrier((gram, acc))
    inverse, scaled = factor_inverse(core_of, gram, swap(gram), float(total_rows) ** 0.5)
    basis = basis_of(own, scaled)

    far_top, far_bot, inverse = lax.optimization_barrier((far_top, far_bot, inverse))
    weights = weigh([far_top, far_bot], [far], [(0, 0, 0, 0), (1, 0, 0, 1)], acc)
    weights = project(core_of, inverse, *weights)
    parts = lax.all_to_all(weights, ("y", "z", "core"), 0, 0, tiled=True)
    return basis, jnp.sum(parts.reshape(-1, rank // 16, rank), 0)


def solution(mesh):
    fine = Mesh(mesh.devices.reshape(4, 4, 4, 2), AXES)
    return jax.shard_map(
        shards,
        mesh=fine,
        in_specs=(P(("y", "z"), ("x", "core")), P(("x", "core"), None), P(AXES, None)),
        out_specs=(P(AXES, None), P(("y", "z"), ("x", "core"))),
        check_vma=False,
    )
```

```python
import functools

import jax
import jax.numpy as jnp
from jax import lax
from jax.experimental import pallas as pl
from jax.experimental.pallas import tpu as pltpu
from jax.sharding import Mesh, PartitionSpec as P

AXES = ("y", "z", "x", "core")
F32 = jnp.float32
BF16 = jnp.bfloat16
LIMIT = 16 * 1024 * 1024
COST = pl.CostEstimate(flops=0, bytes_accessed=0, transcendentals=0)
FIRST = pl.CostEstimate(flops=0, bytes_accessed=0, transcendentals=0)
SLOW = pl.CostEstimate(flops=2 * 10**9, bytes_accessed=0, transcendentals=0)
PARAMS = pltpu.CompilerParams(vmem_limit_bytes=LIMIT)
WHOLE = pl.BlockSpec(memory_space=pltpu.VMEM)


def shift(block, axis, by):
    n = lax.axis_size(axis)
    return lax.ppermute(block, axis, [(i, (i + by) % n) for i in range(n)])


def swap(block):
    return shift(block, "core", 1)


def axis_sum(block, axis):
    far, right, left = (shift(block, axis, by) for by in (2, 1, 3))
    return block + right + left + far


def split(block):
    high = block.astype(BF16)
    return high, (block - high.astype(F32)).astype(BF16)


def mm(a, b):
    return jnp.dot(a, b, preferred_element_type=F32)


def fetch_body(panel_ref, *rest, plan):
    outs, sems = rest[: len(plan)], rest[len(plan)]
    rows = outs[0].shape[0]
    x = lax.axis_index("x")
    core = lax.axis_index("core")
    copies = []
    for slot, (step, other) in enumerate(plan):
        chunk = lax.rem(x + step, 4) * 2 + (1 - core if other else core)
        start = pl.multiple_of(chunk * rows, rows)
        copies.append(
            pltpu.make_async_copy(panel_ref.at[pl.ds(start, rows), :], outs[slot], sems.at[slot])
        )
    for copy in copies:
        copy.start()
    for copy in copies:
        copy.wait()


def fetch(panel, rows, *plan):
    count = len(plan)
    cols = panel.shape[1]
    return pl.pallas_call(
        functools.partial(fetch_body, plan=plan),
        out_shape=[pltpu.VMEM((rows, cols), F32)] * count,
        in_specs=[pl.BlockSpec(memory_space=pl.ANY)],
        out_specs=[WHOLE] * count,
        scratch_shapes=[pltpu.SemaphoreType.DMA((count,))],
        compiler_params=PARAMS,
        cost_estimate=COST,
        name="fetch",
    )(panel)


def term_body(mine_ref, other_ref, test_ref, test_other_ref, *rest, first, sizes, block):
    rank = test_ref.shape[1]
    tests = jnp.concatenate([test_ref[...], test_other_ref[...]], 0)
    tests = jnp.concatenate(split(tests), 1)
    out_ref = rest[-1]
    for at in range(0, out_ref.shape[0], block):
        here = slice(first + at, first + at + block)
        high, low = split(jnp.concatenate([mine_ref[here, :], other_ref[here, :]], 1))
        both = mm(low, tests) + mm(high, tests)
        total = both[:, rank:] + both[:, :rank]
        slot = 0
        for size in sizes:
            addend_ref = rest[slot + at // (out_ref.shape[0] // size)]
            begin = at % (out_ref.shape[0] // size)
            total = total + addend_ref[begin : begin + block, :]
            slot += size
        out_ref[at : at + block, :] = total


def term(chunk, first, count, tests, *addends, block=384, cost=COST):
    rank = tests[0].shape[1]
    sizes = tuple(len(parts) for parts in addends)
    return pl.pallas_call(
        functools.partial(term_body, first=first, sizes=sizes, block=block),
        out_shape=pltpu.VMEM((count, rank), F32),
        in_specs=[WHOLE] * (4 + sum(sizes)),
        out_specs=WHOLE,
        compiler_params=PARAMS,
        cost_estimate=cost,
        name="term",
    )(*chunk, *tests, *(array for parts in addends for array in parts))


def finish_body(base_ref, top_ref, bot_ref, own_ref, turned_ref):
    parts, _, size = turned_ref.shape
    for part in range(parts):
        span = slice(part * size, (part + 1) * size)
        both_ref = top_ref if part < parts // 2 else bot_ref
        begin = part % (parts // 2) * size
        own = base_ref[span, :] + both_ref[begin : begin + size, :]
        own_ref[span, :] = own
        turned_ref[part] = own.T


def finish(base, top, bot, parts=2):
    rows, rank = base.shape
    return pl.pallas_call(
        finish_body,
        out_shape=(
            pltpu.VMEM((rows, rank), F32),
            pltpu.VMEM((parts, rank, rows // parts), F32),
        ),
        in_specs=[WHOLE] * 3,
        out_specs=(WHOLE, WHOLE),
        compiler_params=PARAMS,
        cost_estimate=COST,
        name="finish",
    )(base, top, bot)


def gram_body(own_ref, turned_ref, gram_ref):
    parts, _, size = turned_ref.shape
    dot = functools.partial(jnp.dot, precision=lax.Precision.HIGHEST, preferred_element_type=F32)
    total = None
    for part in range(parts):
        piece = dot(turned_ref[part], own_ref[part * size : (part + 1) * size, :])
        total = piece if total is None else total + piece
    gram_ref[...] = total


def gram_of(own, turned):
    rank = own.shape[1]
    return pl.pallas_call(
        gram_body,
        out_shape=pltpu.VMEM((rank, rank), F32),
        in_specs=[WHOLE] * 2,
        out_specs=WHOLE,
        compiler_params=PARAMS,
        cost_estimate=COST,
        name="gram",
    )(own, turned)


def gather_body(*refs):
    keep_ref, give_ref = refs[-2:]
    half = keep_ref.shape[0]
    core = lax.axis_index("core")
    for out_ref, part in ((keep_ref, core), (give_ref, 1 - core)):
        here = pl.ds(pl.multiple_of(part * half, half), half)
        total = refs[0][here, :]
        for ref in refs[1:-2]:
            total = total + ref[here, :]
        out_ref[...] = total


def gather(*parts):
    rank = parts[0].shape[1]
    return pl.pallas_call(
        gather_body,
        out_shape=(pltpu.VMEM((rank // 2, rank), F32),) * 2,
        in_specs=[WHOLE] * len(parts),
        out_specs=(WHOLE, WHOLE),
        compiler_params=PARAMS,
        cost_estimate=COST,
        name="gather",
    )(*parts)


def factor_body(mine_ref, other_ref, inverse_ref, turned_ref, *, scale, tile=8):
    half, n = mine_ref.shape
    blocks = n // tile
    first = lax.axis_index("core") == 0
    upper = jnp.where(first, mine_ref[...], other_ref[...])
    lower = jnp.where(first, other_ref[...], mine_ref[...])
    gram = jnp.concatenate([upper, lower], 0)
    row = lax.broadcasted_iota(jnp.int32, (tile, n), 0)
    lane = lax.broadcasted_iota(jnp.int32, (tile, n), 1)
    mat = [gram[tile * r : tile * (r + 1), :] for r in range(blocks)]
    out = [jnp.where(lane == row + tile * r, 1.0, 0.0).astype(F32) for r in range(blocks)]
    for b in range(blocks):
        live = range(b, blocks)
        col = [
            {r: jnp.broadcast_to(mat[r][:, tile * b + s : tile * b + s + 1], (tile, n)) for r in live}
            for s in range(tile)
        ]
        inv = []
        for s in range(tile):
            inv.append(lax.rsqrt(col[s][b][s : s + 1, :]))
            for r in live:
                col[s][r] = col[s][r] * inv[s]
            for t in range(s + 1, tile):
                factor = col[s][b][t : t + 1, :]
                for r in live:
                    col[t][r] = col[t][r] - col[s][r] * factor
        top, left = mat[b], out[b]
        tops, lefts = [], []
        for s in range(tile):
            tops.append(top[s : s + 1, :] * inv[s])
            lefts.append(left[s : s + 1, :] * inv[s])
            if s + 1 < tile:
                low = jnp.where(row > s, col[s][b], 0.0)
                top = top - low * tops[s]
                left = left - low * lefts[s]
        inverse_ref[tile * b : tile * (b + 1), :] = jnp.concatenate(lefts, 0)
        for r in range(b + 1, blocks):
            for s in range(tile):
                mat[r] = mat[r] - col[s][r] * tops[s]
                out[r] = out[r] - col[s][r] * lefts[s]
    turned_ref[...] = inverse_ref[...].T * scale


def factor_inverse(mine, other, scale):
    rank = mine.shape[1]
    out = jax.ShapeDtypeStruct((rank, rank), F32)
    return pl.pallas_call(
        functools.partial(factor_body, scale=scale),
        out_shape=(out, out),
        in_specs=[WHOLE, WHOLE],
        out_specs=(WHOLE, WHOLE),
        compiler_params=PARAMS,
        cost_estimate=SLOW,
        name="factor",
    )(mine, other)


def basis_body(own_ref, turned_ref, basis_ref):
    basis_ref[...] = jnp.dot(
        own_ref[...], turned_ref[...], precision=lax.Precision.HIGHEST, preferred_element_type=F32
    )


def basis_of(own, turned):
    rows, rank = own.shape
    block = rows // 4
    return pl.pallas_call(
        basis_body,
        out_shape=jax.ShapeDtypeStruct((rows, rank), F32),
        grid=(rows // block,),
        in_specs=[
            pl.BlockSpec((block, rank), lambda i: (i, 0)),
            pl.BlockSpec((rank, rank), lambda i: (0, 0)),
        ],
        out_specs=pl.BlockSpec((block, rank), lambda i: (i, 0)),
        compiler_params=PARAMS,
        cost_estimate=COST,
        name="basis",
    )(own, turned)


def weigh_body(*refs, plan, block):
    keep_ref, give_ref = refs[-2:]
    rank, cols = keep_ref.shape
    total = None
    for turned, part, chunk, chunk_part in plan:
        size = refs[turned].shape[2]
        for at in range(0, size, block):
            rows = jnp.concatenate(split(refs[turned][part, :, at : at + block]), 0)
            here = slice(chunk_part * size + at, chunk_part * size + at + block)
            high, low = split(jnp.concatenate([refs[chunk][here, :], refs[chunk + 1][here, :]], 1))
            both = mm(rows, low) + mm(rows, high)
            total = both if total is None else total + both
    total = total[rank:] + total[:rank]
    keep, give = total[:, :cols], total[:, cols:]
    if len(refs) > 2 + max(step[2] for step in plan) + 2:
        keep = refs[-4][...] + keep
        give = refs[-3][...] + give
    keep_ref[...] = keep
    give_ref[...] = give


def weigh(turned, chunks, plan, acc=(), cost=COST, block=384):
    rank = turned[0].shape[1]
    cols = chunks[0][0].shape[1]
    args = list(turned) + [array for chunk in chunks for array in chunk] + list(acc)
    plan = [(t, part, len(turned) + 2 * c, chunk_part) for t, part, c, chunk_part in plan]
    return pl.pallas_call(
        functools.partial(weigh_body, plan=plan, block=block),
        out_shape=(pltpu.VMEM((rank, cols), F32),) * 2,
        in_specs=[WHOLE] * len(args),
        out_specs=(WHOLE, WHOLE),
        compiler_params=PARAMS,
        cost_estimate=cost,
        name="weigh",
    )(*args)


def project_body(inverse_ref, keep_ref, give_ref, out_ref):
    dot = functools.partial(jnp.dot, precision=lax.Precision.HIGHEST, preferred_element_type=F32)
    rank, cols = keep_ref.shape
    keep = dot(inverse_ref[...], keep_ref[...])
    give = dot(inverse_ref[...], give_ref[...])
    first = lax.axis_index("core") == 0
    both = jnp.concatenate([jnp.where(first, keep, give), jnp.where(first, give, keep)], 1)
    for part in range(16):
        span = slice(part * (rank // 16), (part + 1) * (rank // 16))
        out_ref[part, 0] = both[span, :cols]
        out_ref[part, 1] = both[span, cols:]


def project(inverse, keep, give):
    rank, cols = keep.shape
    out = pl.pallas_call(
        project_body,
        out_shape=jax.ShapeDtypeStruct((16, 2, rank // 16, cols), F32),
        in_specs=[WHOLE] * 3,
        out_specs=WHOLE,
        compiler_params=PARAMS,
        cost_estimate=COST,
        name="project",
    )(inverse, keep, give)
    return out.reshape(2 * rank, cols)


def shards(panel, test_matrix, prior_sketch):
    rows, rank = prior_sketch.shape
    half = rows // 2
    total_rows = panel.shape[0] * lax.axis_size("y") * lax.axis_size("z")

    panel = pltpu.with_memory_space_constraint(panel, pltpu.HBM)
    test_other = swap(test_matrix)
    (far_give,) = fetch(panel, rows, (2, 1))
    panel, far_give, test_other = lax.optimization_barrier((panel, far_give, test_other))
    tests = (test_matrix, test_other)
    far_other = swap(far_give)
    far_keep, right_keep, left_keep, here_keep, *give = fetch(
        panel, rows, (2, 0), (1, 0), (3, 0), (0, 0), (1, 1), (3, 1), (0, 1)
    )
    far = (far_keep, far_other)
    far_top = term(far, 0, half, tests)
    far_bot = term(far, half, half, tests)
    far_top, far_bot, *give = lax.optimization_barrier((far_top, far_bot, *give))
    far_top = shift(far_top, "x", 1)
    far_bot = shift(far_bot, "x", 3)
    right = (right_keep, swap(give[0]))
    left = (left_keep, swap(give[1]))
    near_bot = term(right, half, half, tests)
    near_top = term(left, 0, half, tests)
    near_bot, near_top, here_give = lax.optimization_barrier((near_bot, near_top, give[2]))
    near_bot = shift(near_bot, "x", 1)
    near_top = shift(near_top, "x", 3)
    here = (here_keep, swap(here_give))
    base = term(here, 0, rows, tests, (prior_sketch,), (near_top, near_bot), cost=FIRST)
    far_top, far_bot = lax.optimization_barrier((far_top, far_bot))
    both_top = shift(term(right, 0, half, tests, (far_top,)), "x", 1)
    both_bot = shift(term(left, half, half, tests, (far_bot,)), "x", 3)
    own, turned = finish(base, both_top, both_bot)

    from_left = shift(turned, "x", 1)
    from_right = shift(turned, "x", 3)
    keep, give = gather(gram_of(own, turned))
    gram = keep + swap(give)
    gram = axis_sum(axis_sum(gram, "y"), "z")
    gram, turned = lax.optimization_barrier((gram, turned))
    acc = weigh([turned], [here], [(0, 0, 0, 0), (0, 1, 0, 1)])
    across = [shift(gram, "x", by) for by in (2, 1, 3)]

    acc, from_left, from_right = lax.optimization_barrier((acc, from_left, from_right))
    far_bot = shift(from_left[1:], "x", 1)
    far_top = shift(from_right[:1], "x", 3)
    acc = weigh(
        [from_left, from_right],
        [left, right],
        [(0, 0, 0, 0), (0, 1, 0, 1), (1, 0, 1, 0), (1, 1, 1, 1)],
        acc,
    )
    gram = gram + across[0] + across[1] + across[2]
    gram, acc = lax.optimization_barrier((gram, acc))
    inverse, scaled = factor_inverse(gram, swap(gram), float(total_rows) ** 0.5)
    basis = basis_of(own, scaled)

    far_top, far_bot, inverse = lax.optimization_barrier((far_top, far_bot, inverse))
    weights = weigh([far_top, far_bot], [far], [(0, 0, 0, 0), (1, 0, 0, 1)], acc)
    weights = project(inverse, *weights)
    parts = lax.all_to_all(weights, ("y", "z", "core"), 0, 0, tiled=True)
    return basis, jnp.sum(parts.reshape(-1, rank // 16, rank), 0)


def solution(mesh):
    fine = Mesh(mesh.devices.reshape(4, 4, 4, 2), AXES)
    return jax.shard_map(
        shards,
        mesh=fine,
        in_specs=(P(("y", "z"), ("x", "core")), P(("x", "core"), None), P(AXES, None)),
        out_specs=(P(AXES, None), P(("y", "z"), ("x", "core"))),
        check_vma=False,
    )
```

```python
import functools

import jax
import jax.numpy as jnp
from jax import lax
from jax.experimental import pallas as pl
from jax.experimental.pallas import tpu as pltpu
from jax.sharding import Mesh, PartitionSpec as P

AXES = ("y", "z", "x", "core")
F32 = jnp.float32
BF16 = jnp.bfloat16
LIMIT = 16 * 1024 * 1024
COST = pl.CostEstimate(flops=0, bytes_accessed=0, transcendentals=0)
FIRST = pl.CostEstimate(flops=3 * 10**8, bytes_accessed=0, transcendentals=0)
SLOW = pl.CostEstimate(flops=13 * 10**8, bytes_accessed=0, transcendentals=0)
PARAMS = pltpu.CompilerParams(vmem_limit_bytes=LIMIT)
WHOLE = pl.BlockSpec(memory_space=pltpu.VMEM)


def shift(block, axis, by):
    n = lax.axis_size(axis)
    return lax.ppermute(block, axis, [(i, (i + by) % n) for i in range(n)])


def swap(block):
    return shift(block, "core", 1)


def axis_sum(block, axis):
    far, right, left = (shift(block, axis, by) for by in (2, 1, 3))
    return block + right + left + far


def split(block):
    high = block.astype(BF16)
    return high, (block - high.astype(F32)).astype(BF16)


def mm(a, b):
    return jnp.dot(a, b, preferred_element_type=F32)


def fetch_body(panel_ref, *rest, plan):
    outs, sems = rest[: len(plan)], rest[len(plan)]
    rows = outs[0].shape[0]
    x = lax.axis_index("x")
    core = lax.axis_index("core")
    copies = []
    for slot, (step, other) in enumerate(plan):
        chunk = lax.rem(x + step, 4) * 2 + (1 - core if other else core)
        start = pl.multiple_of(chunk * rows, rows)
        copies.append(
            pltpu.make_async_copy(panel_ref.at[pl.ds(start, rows), :], outs[slot], sems.at[slot])
        )
    for copy in copies:
        copy.start()
    for copy in copies:
        copy.wait()


def fetch(panel, rows, *plan):
    count = len(plan)
    cols = panel.shape[1]
    return pl.pallas_call(
        functools.partial(fetch_body, plan=plan),
        out_shape=[pltpu.VMEM((rows, cols), F32)] * count,
        in_specs=[pl.BlockSpec(memory_space=pl.ANY)],
        out_specs=[WHOLE] * count,
        scratch_shapes=[pltpu.SemaphoreType.DMA((count,))],
        compiler_params=PARAMS,
        cost_estimate=COST,
        name="fetch",
    )(panel)


def term_body(mine_ref, other_ref, test_ref, test_other_ref, *rest, first, sizes, block):
    rank = test_ref.shape[1]
    tests = jnp.concatenate([test_ref[...], test_other_ref[...]], 0)
    tests = jnp.concatenate(split(tests), 1)
    out_ref = rest[-1]
    for at in range(0, out_ref.shape[0], block):
        here = slice(first + at, first + at + block)
        high, low = split(jnp.concatenate([mine_ref[here, :], other_ref[here, :]], 1))
        both = mm(low, tests) + mm(high, tests)
        total = both[:, rank:] + both[:, :rank]
        slot = 0
        for size in sizes:
            addend_ref = rest[slot + at // (out_ref.shape[0] // size)]
            begin = at % (out_ref.shape[0] // size)
            total = total + addend_ref[begin : begin + block, :]
            slot += size
        out_ref[at : at + block, :] = total


def term(chunk, first, count, tests, *addends, block=384, cost=COST):
    rank = tests[0].shape[1]
    sizes = tuple(len(parts) for parts in addends)
    return pl.pallas_call(
        functools.partial(term_body, first=first, sizes=sizes, block=block),
        out_shape=pltpu.VMEM((count, rank), F32),
        in_specs=[WHOLE] * (4 + sum(sizes)),
        out_specs=WHOLE,
        compiler_params=PARAMS,
        cost_estimate=cost,
        name="term",
    )(*chunk, *tests, *(array for parts in addends for array in parts))


def finish_body(base_ref, top_ref, bot_ref, own_ref, turned_ref):
    parts, _, size = turned_ref.shape
    for part in range(parts):
        span = slice(part * size, (part + 1) * size)
        both_ref = top_ref if part < parts // 2 else bot_ref
        begin = part % (parts // 2) * size
        own = base_ref[span, :] + both_ref[begin : begin + size, :]
        own_ref[span, :] = own
        turned_ref[part] = own.T


def finish(base, top, bot, parts=2):
    rows, rank = base.shape
    return pl.pallas_call(
        finish_body,
        out_shape=(
            pltpu.VMEM((rows, rank), F32),
            pltpu.VMEM((parts, rank, rows // parts), F32),
        ),
        in_specs=[WHOLE] * 3,
        out_specs=(WHOLE, WHOLE),
        compiler_params=PARAMS,
        cost_estimate=COST,
        name="finish",
    )(base, top, bot)


def gram_body(own_ref, turned_ref, gram_ref):
    parts, _, size = turned_ref.shape
    dot = functools.partial(jnp.dot, precision=lax.Precision.HIGHEST, preferred_element_type=F32)
    total = None
    for part in range(parts):
        piece = dot(turned_ref[part], own_ref[part * size : (part + 1) * size, :])
        total = piece if total is None else total + piece
    gram_ref[...] = total


def gram_of(own, turned):
    rank = own.shape[1]
    return pl.pallas_call(
        gram_body,
        out_shape=pltpu.VMEM((rank, rank), F32),
        in_specs=[WHOLE] * 2,
        out_specs=WHOLE,
        compiler_params=PARAMS,
        cost_estimate=COST,
        name="gram",
    )(own, turned)


def gather_body(*refs):
    keep_ref, give_ref = refs[-2:]
    half = keep_ref.shape[0]
    core = lax.axis_index("core")
    for out_ref, part in ((keep_ref, core), (give_ref, 1 - core)):
        here = pl.ds(pl.multiple_of(part * half, half), half)
        total = refs[0][here, :]
        for ref in refs[1:-2]:
            total = total + ref[here, :]
        out_ref[...] = total


def gather(*parts):
    rank = parts[0].shape[1]
    return pl.pallas_call(
        gather_body,
        out_shape=(pltpu.VMEM((rank // 2, rank), F32),) * 2,
        in_specs=[WHOLE] * len(parts),
        out_specs=(WHOLE, WHOLE),
        compiler_params=PARAMS,
        cost_estimate=COST,
        name="gather",
    )(*parts)


def factor_body(mine_ref, other_ref, inverse_ref, turned_ref, *, scale, tile=8):
    half, n = mine_ref.shape
    blocks = n // tile
    first = lax.axis_index("core") == 0
    upper = jnp.where(first, mine_ref[...], other_ref[...])
    lower = jnp.where(first, other_ref[...], mine_ref[...])
    gram = jnp.concatenate([upper, lower], 0)
    row = lax.broadcasted_iota(jnp.int32, (tile, n), 0)
    lane = lax.broadcasted_iota(jnp.int32, (tile, n), 1)
    mat = [gram[tile * r : tile * (r + 1), :] for r in range(blocks)]
    out = [jnp.where(lane == row + tile * r, 1.0, 0.0).astype(F32) for r in range(blocks)]
    for b in range(blocks):
        live = range(b, blocks)
        col = [
            {r: jnp.broadcast_to(mat[r][:, tile * b + s : tile * b + s + 1], (tile, n)) for r in live}
            for s in range(tile)
        ]
        inv = []
        for s in range(tile):
            inv.append(lax.rsqrt(col[s][b][s : s + 1, :]))
            for r in live:
                col[s][r] = col[s][r] * inv[s]
            for t in range(s + 1, tile):
                factor = col[s][b][t : t + 1, :]
                for r in live:
                    col[t][r] = col[t][r] - col[s][r] * factor
        top, left = mat[b], out[b]
        tops, lefts = [], []
        for s in range(tile):
            tops.append(top[s : s + 1, :] * inv[s])
            lefts.append(left[s : s + 1, :] * inv[s])
            if s + 1 < tile:
                low = jnp.where(row > s, col[s][b], 0.0)
                top = top - low * tops[s]
                left = left - low * lefts[s]
        inverse_ref[tile * b : tile * (b + 1), :] = jnp.concatenate(lefts, 0)
        for r in range(b + 1, blocks):
            for s in range(tile):
                mat[r] = mat[r] - col[s][r] * tops[s]
                out[r] = out[r] - col[s][r] * lefts[s]
    turned_ref[...] = inverse_ref[...].T * scale


def factor_inverse(mine, other, scale):
    rank = mine.shape[1]
    out = jax.ShapeDtypeStruct((rank, rank), F32)
    return pl.pallas_call(
        functools.partial(factor_body, scale=scale),
        out_shape=(out, out),
        in_specs=[WHOLE, WHOLE],
        out_specs=(WHOLE, WHOLE),
        compiler_params=PARAMS,
        cost_estimate=SLOW,
        name="factor",
    )(mine, other)


def basis_body(own_ref, turned_ref, basis_ref):
    basis_ref[...] = jnp.dot(
        own_ref[...], turned_ref[...], precision=lax.Precision.HIGHEST, preferred_element_type=F32
    )


def basis_of(own, turned):
    rows, rank = own.shape
    block = rows // 4
    return pl.pallas_call(
        basis_body,
        out_shape=jax.ShapeDtypeStruct((rows, rank), F32),
        grid=(rows // block,),
        in_specs=[
            pl.BlockSpec((block, rank), lambda i: (i, 0)),
            pl.BlockSpec((rank, rank), lambda i: (0, 0)),
        ],
        out_specs=pl.BlockSpec((block, rank), lambda i: (i, 0)),
        compiler_params=PARAMS,
        cost_estimate=COST,
        name="basis",
    )(own, turned)


def weigh_body(*refs, plan, block, width):
    total = None
    for turned, part, chunk, chunk_part in plan:
        size = refs[turned].shape[2]
        for at in range(0, size, block):
            rows = jnp.concatenate(split(refs[turned][part, :, at : at + block]), 0)
            here = slice(chunk_part * size + at, chunk_part * size + at + block)
            high, low = split(jnp.concatenate([refs[chunk][here, :], refs[chunk + 1][here, :]], 1))
            both = mm(rows, low) + mm(rows, high)
            total = both if total is None else total + both
    rank = total.shape[0] // 2
    total = total[rank:] + total[:rank]
    extra = refs[width:]
    if len(extra) > 1:
        total = extra[0][...] + total
    if len(extra) < 3:
        extra[-1][...] = total
        return
    total = jnp.dot(
        extra[1][...], total, precision=lax.Precision.HIGHEST, preferred_element_type=F32
    )
    first = lax.axis_index("core") == 0
    cols = rank
    keep, give = total[:, :cols], total[:, cols:]
    low_core = jnp.where(first, keep, give)
    high_core = jnp.where(first, give, keep)
    out_ref = extra[2]
    for part in range(out_ref.shape[0]):
        span = slice(part * (rank // 16), (part + 1) * (rank // 16))
        out_ref[part, 0] = low_core[span]
        out_ref[part, 1] = high_core[span]


def weigh(turned, chunks, plan, acc=None, inverse=None, block=384):
    rank = turned[0].shape[1]
    cols = chunks[0][0].shape[1]
    args = list(turned) + [array for chunk in chunks for array in chunk]
    width = len(args)
    args += [array for array in (acc, inverse) if array is not None]
    plan = [(t, part, len(turned) + 2 * c, chunk_part) for t, part, c, chunk_part in plan]
    if inverse is None:
        out = pltpu.VMEM((rank, 2 * cols), F32)
    else:
        out = jax.ShapeDtypeStruct((16, 2, rank // 16, cols), F32)
    return pl.pallas_call(
        functools.partial(weigh_body, plan=plan, block=block, width=width),
        out_shape=out,
        in_specs=[WHOLE] * len(args),
        out_specs=WHOLE,
        compiler_params=PARAMS,
        cost_estimate=COST,
        name="weigh",
    )(*args)


def shards(panel, test_matrix, prior_sketch):
    rows, rank = prior_sketch.shape
    half = rows // 2
    total_rows = panel.shape[0] * lax.axis_size("y") * lax.axis_size("z")

    panel = pltpu.with_memory_space_constraint(panel, pltpu.HBM)
    test_other = swap(test_matrix)
    (far_give,) = fetch(panel, rows, (2, 1))
    panel, far_give, test_other = lax.optimization_barrier((panel, far_give, test_other))
    tests = (test_matrix, test_other)
    far_other = swap(far_give)
    far_keep, right_keep, left_keep, here_keep, *give = fetch(
        panel, rows, (2, 0), (1, 0), (3, 0), (0, 0), (1, 1), (3, 1), (0, 1)
    )
    far = (far_keep, far_other)
    far_top = term(far, 0, half, tests)
    far_bot = term(far, half, half, tests)
    far_top, far_bot, *give = lax.optimization_barrier((far_top, far_bot, *give))
    far_top = shift(far_top, "x", 1)
    far_bot = shift(far_bot, "x", 3)
    right = (right_keep, swap(give[0]))
    left = (left_keep, swap(give[1]))
    near_bot = term(right, half, half, tests)
    near_top = term(left, 0, half, tests)
    near_bot, near_top = lax.optimization_barrier((near_bot, near_top))
    near_bot = shift(near_bot, "x", 1)
    near_top = shift(near_top, "x", 3)
    here = (here_keep, swap(give[2]))
    base = term(here, 0, rows, tests, (prior_sketch,), (near_top, near_bot), cost=FIRST)
    far_top, far_bot = lax.optimization_barrier((far_top, far_bot))
    both_top = shift(term(right, 0, half, tests, (far_top,)), "x", 1)
    both_bot = shift(term(left, half, half, tests, (far_bot,)), "x", 3)
    own, turned = finish(base, both_top, both_bot)

    from_left = shift(turned, "x", 1)
    from_right = shift(turned, "x", 3)
    keep, give = gather(gram_of(own, turned))
    gram = keep + swap(give)
    gram = axis_sum(axis_sum(gram, "y"), "z")
    gram, turned = lax.optimization_barrier((gram, turned))
    acc = weigh([turned], [here], [(0, 0, 0, 0), (0, 1, 0, 1)])
    across = [shift(gram, "x", by) for by in (2, 1, 3)]

    acc, from_left, from_right = lax.optimization_barrier((acc, from_left, from_right))
    far_bot = shift(from_left[1:], "x", 1)
    far_top = shift(from_right[:1], "x", 3)
    acc = weigh(
        [from_left, from_right],
        [left, right],
        [(0, 0, 0, 0), (0, 1, 0, 1), (1, 0, 1, 0), (1, 1, 1, 1)],
        acc,
    )
    acc, across = lax.optimization_barrier((acc, across))
    gram = gram + across[0] + across[1] + across[2]
    inverse, scaled = factor_inverse(gram, swap(gram), float(total_rows) ** 0.5)
    basis = basis_of(own, scaled)

    far_top, far_bot, inverse = lax.optimization_barrier((far_top, far_bot, inverse))
    weights = weigh([far_top, far_bot], [far], [(0, 0, 0, 0), (1, 0, 0, 1)], acc, inverse)
    parts = lax.all_to_all(weights.reshape(2 * rank, -1), ("y", "z", "core"), 0, 0, tiled=True)
    return basis, jnp.sum(parts.reshape(-1, rank // 16, rank), 0)


def solution(mesh):
    fine = Mesh(mesh.devices.reshape(4, 4, 4, 2), AXES)
    return jax.shard_map(
        shards,
        mesh=fine,
        in_specs=(P(("y", "z"), ("x", "core")), P(("x", "core"), None), P(AXES, None)),
        out_specs=(P(AXES, None), P(("y", "z"), ("x", "core"))),
        check_vma=False,
    )
```

```python
import functools

import jax
import jax.numpy as jnp
from jax import lax
from jax.experimental import pallas as pl
from jax.experimental.pallas import tpu as pltpu
from jax.sharding import Mesh, PartitionSpec as P

AXES = ("y", "z", "x", "core")
F32 = jnp.float32
BF16 = jnp.bfloat16
LIMIT = 16 * 1024 * 1024
COST = pl.CostEstimate(flops=0, bytes_accessed=0, transcendentals=0)
FIRST = pl.CostEstimate(flops=3 * 10**8, bytes_accessed=0, transcendentals=0)
SLOW = pl.CostEstimate(flops=13 * 10**8, bytes_accessed=0, transcendentals=0)
PARAMS = pltpu.CompilerParams(vmem_limit_bytes=LIMIT)
WHOLE = pl.BlockSpec(memory_space=pltpu.VMEM)


def shift(block, axis, by):
    n = lax.axis_size(axis)
    return lax.ppermute(block, axis, [(i, (i + by) % n) for i in range(n)])


def swap(block):
    return shift(block, "core", 1)


def axis_sum(block, axis):
    far, right, left = (shift(block, axis, by) for by in (2, 1, 3))
    return block + right + left + far


def split(block):
    high = block.astype(BF16)
    return high, (block - high.astype(F32)).astype(BF16)


def mm(a, b):
    return jnp.dot(a, b, preferred_element_type=F32)


def fetch_body(panel_ref, *rest, plan):
    outs, sems = rest[: len(plan)], rest[len(plan)]
    rows = outs[0].shape[0]
    x = lax.axis_index("x")
    core = lax.axis_index("core")
    copies = []
    for slot, (step, other) in enumerate(plan):
        chunk = lax.rem(x + step, 4) * 2 + (1 - core if other else core)
        start = pl.multiple_of(chunk * rows, rows)
        copies.append(
            pltpu.make_async_copy(panel_ref.at[pl.ds(start, rows), :], outs[slot], sems.at[slot])
        )
    for copy in copies:
        copy.start()
    for copy in copies:
        copy.wait()


def fetch(panel, rows, *plan):
    count = len(plan)
    cols = panel.shape[1]
    return pl.pallas_call(
        functools.partial(fetch_body, plan=plan),
        out_shape=[pltpu.VMEM((rows, cols), F32)] * count,
        in_specs=[pl.BlockSpec(memory_space=pl.ANY)],
        out_specs=[WHOLE] * count,
        scratch_shapes=[pltpu.SemaphoreType.DMA((count,))],
        compiler_params=PARAMS,
        cost_estimate=COST,
        name="fetch",
    )(panel)


def term_body(mine_ref, other_ref, test_ref, test_other_ref, *rest, first, sizes, block):
    rank = test_ref.shape[1]
    tests = jnp.concatenate([test_ref[...], test_other_ref[...]], 0)
    tests = jnp.concatenate(split(tests), 1)
    out_ref = rest[-1]
    for at in range(0, out_ref.shape[0], block):
        here = slice(first + at, first + at + block)
        high, low = split(jnp.concatenate([mine_ref[here, :], other_ref[here, :]], 1))
        both = mm(low, tests) + mm(high, tests)
        total = both[:, rank:] + both[:, :rank]
        slot = 0
        for size in sizes:
            addend_ref = rest[slot + at // (out_ref.shape[0] // size)]
            begin = at % (out_ref.shape[0] // size)
            total = total + addend_ref[begin : begin + block, :]
            slot += size
        out_ref[at : at + block, :] = total


def term(chunk, first, count, tests, *addends, block=384, cost=COST):
    rank = tests[0].shape[1]
    sizes = tuple(len(parts) for parts in addends)
    return pl.pallas_call(
        functools.partial(term_body, first=first, sizes=sizes, block=block),
        out_shape=pltpu.VMEM((count, rank), F32),
        in_specs=[WHOLE] * (4 + sum(sizes)),
        out_specs=WHOLE,
        compiler_params=PARAMS,
        cost_estimate=cost,
        name="term",
    )(*chunk, *tests, *(array for parts in addends for array in parts))


def finish_body(base_ref, top_ref, bot_ref, own_ref, turned_ref):
    parts, _, size = turned_ref.shape
    for part in range(parts):
        span = slice(part * size, (part + 1) * size)
        both_ref = top_ref if part < parts // 2 else bot_ref
        begin = part % (parts // 2) * size
        own = base_ref[span, :] + both_ref[begin : begin + size, :]
        own_ref[span, :] = own
        turned_ref[part] = own.T


def finish(base, top, bot, parts=2):
    rows, rank = base.shape
    return pl.pallas_call(
        finish_body,
        out_shape=(
            pltpu.VMEM((rows, rank), F32),
            pltpu.VMEM((parts, rank, rows // parts), F32),
        ),
        in_specs=[WHOLE] * 3,
        out_specs=(WHOLE, WHOLE),
        compiler_params=PARAMS,
        cost_estimate=COST,
        name="finish",
    )(base, top, bot)


def gram_body(own_ref, turned_ref, gram_ref):
    parts, _, size = turned_ref.shape
    dot = functools.partial(jnp.dot, precision=lax.Precision.HIGHEST, preferred_element_type=F32)
    total = None
    for part in range(parts):
        piece = dot(turned_ref[part], own_ref[part * size : (part + 1) * size, :])
        total = piece if total is None else total + piece
    gram_ref[...] = total


def gram_of(own, turned):
    rank = own.shape[1]
    return pl.pallas_call(
        gram_body,
        out_shape=pltpu.VMEM((rank, rank), F32),
        in_specs=[WHOLE] * 2,
        out_specs=WHOLE,
        compiler_params=PARAMS,
        cost_estimate=COST,
        name="gram",
    )(own, turned)


def gather_body(*refs):
    keep_ref, give_ref = refs[-2:]
    half = keep_ref.shape[0]
    core = lax.axis_index("core")
    for out_ref, part in ((keep_ref, core), (give_ref, 1 - core)):
        here = pl.ds(pl.multiple_of(part * half, half), half)
        total = refs[0][here, :]
        for ref in refs[1:-2]:
            total = total + ref[here, :]
        out_ref[...] = total


def gather(*parts):
    rank = parts[0].shape[1]
    return pl.pallas_call(
        gather_body,
        out_shape=(pltpu.VMEM((rank // 2, rank), F32),) * 2,
        in_specs=[WHOLE] * len(parts),
        out_specs=(WHOLE, WHOLE),
        compiler_params=PARAMS,
        cost_estimate=COST,
        name="gather",
    )(*parts)


def factor_body(mine_ref, other_ref, inverse_ref, turned_ref, *, scale, tile=8):
    half, n = mine_ref.shape
    blocks = n // tile
    first = lax.axis_index("core") == 0
    upper = jnp.where(first, mine_ref[...], other_ref[...])
    lower = jnp.where(first, other_ref[...], mine_ref[...])
    gram = jnp.concatenate([upper, lower], 0)
    row = lax.broadcasted_iota(jnp.int32, (tile, n), 0)
    lane = lax.broadcasted_iota(jnp.int32, (tile, n), 1)
    mat = [gram[tile * r : tile * (r + 1), :] for r in range(blocks)]
    out = [jnp.where(lane == row + tile * r, 1.0, 0.0).astype(F32) for r in range(blocks)]
    for b in range(blocks):
        live = range(b, blocks)
        col = [
            {r: jnp.broadcast_to(mat[r][:, tile * b + s : tile * b + s + 1], (tile, n)) for r in live}
            for s in range(tile)
        ]
        inv = []
        for s in range(tile):
            inv.append(lax.rsqrt(col[s][b][s : s + 1, :]))
            for r in live:
                col[s][r] = col[s][r] * inv[s]
            for t in range(s + 1, tile):
                factor = col[s][b][t : t + 1, :]
                for r in live:
                    col[t][r] = col[t][r] - col[s][r] * factor
        top, left = mat[b], out[b]
        tops, lefts = [], []
        for s in range(tile):
            tops.append(top[s : s + 1, :] * inv[s])
            lefts.append(left[s : s + 1, :] * inv[s])
            if s + 1 < tile:
                low = jnp.where(row > s, col[s][b], 0.0)
                top = top - low * tops[s]
                left = left - low * lefts[s]
        inverse_ref[tile * b : tile * (b + 1), :] = jnp.concatenate(lefts, 0)
        for r in range(b + 1, blocks):
            for s in range(tile):
                mat[r] = mat[r] - col[s][r] * tops[s]
                out[r] = out[r] - col[s][r] * lefts[s]
    turned_ref[...] = inverse_ref[...].T * scale


def factor_inverse(mine, other, scale):
    rank = mine.shape[1]
    out = jax.ShapeDtypeStruct((rank, rank), F32)
    return pl.pallas_call(
        functools.partial(factor_body, scale=scale),
        out_shape=(out, out),
        in_specs=[WHOLE, WHOLE],
        out_specs=(WHOLE, WHOLE),
        compiler_params=PARAMS,
        cost_estimate=SLOW,
        name="factor",
    )(mine, other)


def basis_body(own_ref, turned_ref, basis_ref):
    basis_ref[...] = jnp.dot(
        own_ref[...], turned_ref[...], precision=lax.Precision.HIGHEST, preferred_element_type=F32
    )


def basis_of(own, turned):
    rows, rank = own.shape
    block = rows // 4
    return pl.pallas_call(
        basis_body,
        out_shape=jax.ShapeDtypeStruct((rows, rank), F32),
        grid=(rows // block,),
        in_specs=[
            pl.BlockSpec((block, rank), lambda i: (i, 0)),
            pl.BlockSpec((rank, rank), lambda i: (0, 0)),
        ],
        out_specs=pl.BlockSpec((block, rank), lambda i: (i, 0)),
        compiler_params=PARAMS,
        cost_estimate=COST,
        name="basis",
    )(own, turned)


def weigh_body(*refs, plan, block, width):
    total = None
    for turned, part, chunk, chunk_part in plan:
        size = refs[turned].shape[2]
        for at in range(0, size, block):
            rows = jnp.concatenate(split(refs[turned][part, :, at : at + block]), 0)
            here = slice(chunk_part * size + at, chunk_part * size + at + block)
            high, low = split(jnp.concatenate([refs[chunk][here, :], refs[chunk + 1][here, :]], 1))
            both = mm(rows, low) + mm(rows, high)
            total = both if total is None else total + both
    rank = total.shape[0] // 2
    total = total[rank:] + total[:rank]
    extra = refs[width:]
    if len(extra) > 1:
        total = extra[0][...] + total
    if len(extra) < 3:
        extra[-1][...] = total
        return
    total = jnp.dot(
        extra[1][...], total, precision=lax.Precision.HIGHEST, preferred_element_type=F32
    )
    first = lax.axis_index("core") == 0
    cols = rank
    keep, give = total[:, :cols], total[:, cols:]
    low_core = jnp.where(first, keep, give)
    high_core = jnp.where(first, give, keep)
    out_ref = extra[2]
    for part in range(out_ref.shape[0]):
        span = slice(part * (rank // 16), (part + 1) * (rank // 16))
        out_ref[part, 0] = low_core[span]
        out_ref[part, 1] = high_core[span]


def weigh(turned, chunks, plan, acc=None, inverse=None, block=384):
    rank = turned[0].shape[1]
    cols = chunks[0][0].shape[1]
    args = list(turned) + [array for chunk in chunks for array in chunk]
    width = len(args)
    args += [array for array in (acc, inverse) if array is not None]
    plan = [(t, part, len(turned) + 2 * c, chunk_part) for t, part, c, chunk_part in plan]
    if inverse is None:
        out = pltpu.VMEM((rank, 2 * cols), F32)
    else:
        out = jax.ShapeDtypeStruct((16, 2, rank // 16, cols), F32)
    return pl.pallas_call(
        functools.partial(weigh_body, plan=plan, block=block, width=width),
        out_shape=out,
        in_specs=[WHOLE] * len(args),
        out_specs=WHOLE,
        compiler_params=PARAMS,
        cost_estimate=COST,
        name="weigh",
    )(*args)


def total_body(parts_ref, out_ref):
    rows = out_ref.shape[0]
    total = parts_ref[:rows, :]
    for at in range(rows, parts_ref.shape[0], rows):
        total = total + parts_ref[at : at + rows, :]
    out_ref[...] = total


def total_of(parts, rows):
    return pl.pallas_call(
        total_body,
        out_shape=jax.ShapeDtypeStruct((rows, parts.shape[1]), F32),
        in_specs=[WHOLE],
        out_specs=WHOLE,
        compiler_params=PARAMS,
        cost_estimate=COST,
        name="total",
    )(parts)


def shards(panel, test_matrix, prior_sketch):
    rows, rank = prior_sketch.shape
    half = rows // 2
    total_rows = panel.shape[0] * lax.axis_size("y") * lax.axis_size("z")

    panel = pltpu.with_memory_space_constraint(panel, pltpu.HBM)
    test_other = swap(test_matrix)
    (far_give,) = fetch(panel, rows, (2, 1))
    panel, far_give, test_other = lax.optimization_barrier((panel, far_give, test_other))
    tests = (test_matrix, test_other)
    far_other = swap(far_give)
    far_keep, right_keep, left_keep, here_keep, *give = fetch(
        panel, rows, (2, 0), (1, 0), (3, 0), (0, 0), (1, 1), (3, 1), (0, 1)
    )
    far = (far_keep, far_other)
    far_top = term(far, 0, half, tests)
    far_bot = term(far, half, half, tests)
    far_top, far_bot, *give = lax.optimization_barrier((far_top, far_bot, *give))
    far_top = shift(far_top, "x", 1)
    far_bot = shift(far_bot, "x", 3)
    right = (right_keep, swap(give[0]))
    left = (left_keep, swap(give[1]))
    near_bot = term(right, half, half, tests)
    near_top = term(left, 0, half, tests)
    near_bot, near_top = lax.optimization_barrier((near_bot, near_top))
    near_bot = shift(near_bot, "x", 1)
    near_top = shift(near_top, "x", 3)
    here = (here_keep, swap(give[2]))
    base = term(here, 0, rows, tests, (prior_sketch,), (near_top, near_bot), cost=FIRST)
    far_top, far_bot = lax.optimization_barrier((far_top, far_bot))
    both_top = shift(term(right, 0, half, tests, (far_top,)), "x", 1)
    both_bot = shift(term(left, half, half, tests, (far_bot,)), "x", 3)
    own, turned = finish(base, both_top, both_bot)

    from_left = shift(turned, "x", 1)
    from_right = shift(turned, "x", 3)
    keep, give = gather(gram_of(own, turned))
    gram = keep + swap(give)
    gram = axis_sum(axis_sum(gram, "y"), "z")
    across = [shift(gram, "x", by) for by in (2, 1, 3)]
    gram, from_left, from_right, turned = lax.optimization_barrier(
        (gram, from_left, from_right, turned)
    )
    far_bot = shift(from_left[1:], "x", 1)
    far_top = shift(from_right[:1], "x", 3)
    acc = weigh(
        [turned, from_left, from_right],
        [here, left, right],
        [(source, part, source, part) for source in range(3) for part in range(2)],
    )
    acc, across = lax.optimization_barrier((acc, across))
    gram = gram + across[0] + across[1] + across[2]
    inverse, scaled = factor_inverse(gram, swap(gram), float(total_rows) ** 0.5)
    basis = basis_of(own, scaled)

    far_top, far_bot, inverse = lax.optimization_barrier((far_top, far_bot, inverse))
    weights = weigh([far_top, far_bot], [far], [(0, 0, 0, 0), (1, 0, 0, 1)], acc, inverse)
    parts = lax.all_to_all(weights.reshape(2 * rank, -1), ("y", "z", "core"), 0, 0, tiled=True)
    return basis, total_of(parts, rank // 16)


def solution(mesh):
    fine = Mesh(mesh.devices.reshape(4, 4, 4, 2), AXES)
    return jax.shard_map(
        shards,
        mesh=fine,
        in_specs=(P(("y", "z"), ("x", "core")), P(("x", "core"), None), P(AXES, None)),
        out_specs=(P(AXES, None), P(("y", "z"), ("x", "core"))),
        check_vma=False,
    )
```

```python
import functools

import jax
import jax.numpy as jnp
from jax import lax
from jax.experimental import pallas as pl
from jax.experimental.pallas import tpu as pltpu
from jax.sharding import Mesh, PartitionSpec as P

AXES = ("y", "z", "x", "core")
F32 = jnp.float32
BF16 = jnp.bfloat16
LIMIT = 16 * 1024 * 1024
COST = pl.CostEstimate(flops=0, bytes_accessed=0, transcendentals=0)
FIRST = pl.CostEstimate(flops=3 * 10**8, bytes_accessed=0, transcendentals=0)
SLOW = pl.CostEstimate(flops=13 * 10**8, bytes_accessed=0, transcendentals=0)
PARAMS = pltpu.CompilerParams(vmem_limit_bytes=LIMIT)
WHOLE = pl.BlockSpec(memory_space=pltpu.VMEM)


def shift(block, axis, by):
    n = lax.axis_size(axis)
    return lax.ppermute(block, axis, [(i, (i + by) % n) for i in range(n)])


def swap(block):
    return shift(block, "core", 1)


def axis_sum(block, axis):
    far, right, left = (shift(block, axis, by) for by in (2, 1, 3))
    return block + right + left + far


def split(block):
    high = block.astype(BF16)
    return high, (block - high.astype(F32)).astype(BF16)


def mm(a, b):
    return jnp.dot(a, b, preferred_element_type=F32)


def fetch_body(panel_ref, *rest, plan):
    outs, sems = rest[: len(plan)], rest[len(plan)]
    rows = outs[0].shape[0]
    x = lax.axis_index("x")
    core = lax.axis_index("core")
    copies = []
    for slot, (step, other) in enumerate(plan):
        chunk = lax.rem(x + step, 4) * 2 + (1 - core if other else core)
        start = pl.multiple_of(chunk * rows, rows)
        copies.append(
            pltpu.make_async_copy(panel_ref.at[pl.ds(start, rows), :], outs[slot], sems.at[slot])
        )
    for copy in copies:
        copy.start()
    for copy in copies:
        copy.wait()


def fetch(panel, rows, *plan):
    count = len(plan)
    cols = panel.shape[1]
    return pl.pallas_call(
        functools.partial(fetch_body, plan=plan),
        out_shape=[pltpu.VMEM((rows, cols), F32)] * count,
        in_specs=[pl.BlockSpec(memory_space=pl.ANY)],
        out_specs=[WHOLE] * count,
        scratch_shapes=[pltpu.SemaphoreType.DMA((count,))],
        compiler_params=PARAMS,
        cost_estimate=COST,
        name="fetch",
    )(panel)


def term_body(mine_ref, other_ref, test_ref, test_other_ref, *rest, first, sizes, block):
    rank = test_ref.shape[1]
    tests = jnp.concatenate([test_ref[...], test_other_ref[...]], 0)
    tests = jnp.concatenate(split(tests), 1)
    out_ref = rest[-1]
    for at in range(0, out_ref.shape[0], block):
        here = slice(first + at, first + at + block)
        high, low = split(jnp.concatenate([mine_ref[here, :], other_ref[here, :]], 1))
        both = mm(low, tests) + mm(high, tests)
        total = both[:, rank:] + both[:, :rank]
        slot = 0
        for size in sizes:
            addend_ref = rest[slot + at // (out_ref.shape[0] // size)]
            begin = at % (out_ref.shape[0] // size)
            total = total + addend_ref[begin : begin + block, :]
            slot += size
        out_ref[at : at + block, :] = total


def term(chunk, first, count, tests, *addends, block=384, cost=COST):
    rank = tests[0].shape[1]
    sizes = tuple(len(parts) for parts in addends)
    return pl.pallas_call(
        functools.partial(term_body, first=first, sizes=sizes, block=block),
        out_shape=pltpu.VMEM((count, rank), F32),
        in_specs=[WHOLE] * (4 + sum(sizes)),
        out_specs=WHOLE,
        compiler_params=PARAMS,
        cost_estimate=cost,
        name="term",
    )(*chunk, *tests, *(array for parts in addends for array in parts))


def finish_body(base_ref, top_ref, bot_ref, own_ref, turned_ref):
    parts, _, size = turned_ref.shape
    for part in range(parts):
        span = slice(part * size, (part + 1) * size)
        both_ref = top_ref if part < parts // 2 else bot_ref
        begin = part % (parts // 2) * size
        own = base_ref[span, :] + both_ref[begin : begin + size, :]
        own_ref[span, :] = own
        turned_ref[part] = own.T


def finish(base, top, bot, parts=2):
    rows, rank = base.shape
    return pl.pallas_call(
        finish_body,
        out_shape=(
            pltpu.VMEM((rows, rank), F32),
            pltpu.VMEM((parts, rank, rows // parts), F32),
        ),
        in_specs=[WHOLE] * 3,
        out_specs=(WHOLE, WHOLE),
        compiler_params=PARAMS,
        cost_estimate=COST,
        name="finish",
    )(base, top, bot)


def gram_body(own_ref, turned_ref, gram_ref):
    parts, _, size = turned_ref.shape
    dot = functools.partial(jnp.dot, precision=lax.Precision.HIGHEST, preferred_element_type=F32)
    total = None
    for part in range(parts):
        piece = dot(turned_ref[part], own_ref[part * size : (part + 1) * size, :])
        total = piece if total is None else total + piece
    gram_ref[...] = total


def gram_of(own, turned):
    rank = own.shape[1]
    return pl.pallas_call(
        gram_body,
        out_shape=pltpu.VMEM((rank, rank), F32),
        in_specs=[WHOLE] * 2,
        out_specs=WHOLE,
        compiler_params=PARAMS,
        cost_estimate=COST,
        name="gram",
    )(own, turned)


def gather_body(*refs):
    keep_ref, give_ref = refs[-2:]
    half = keep_ref.shape[0]
    core = lax.axis_index("core")
    for out_ref, part in ((keep_ref, core), (give_ref, 1 - core)):
        here = pl.ds(pl.multiple_of(part * half, half), half)
        total = refs[0][here, :]
        for ref in refs[1:-2]:
            total = total + ref[here, :]
        out_ref[...] = total


def gather(*parts):
    rank = parts[0].shape[1]
    return pl.pallas_call(
        gather_body,
        out_shape=(pltpu.VMEM((rank // 2, rank), F32),) * 2,
        in_specs=[WHOLE] * len(parts),
        out_specs=(WHOLE, WHOLE),
        compiler_params=PARAMS,
        cost_estimate=COST,
        name="gather",
    )(*parts)


def factor_body(mine_ref, other_ref, inverse_ref, turned_ref, *, scale, tile=8):
    half, n = mine_ref.shape
    blocks = n // tile
    first = lax.axis_index("core") == 0
    upper = jnp.where(first, mine_ref[...], other_ref[...])
    lower = jnp.where(first, other_ref[...], mine_ref[...])
    gram = jnp.concatenate([upper, lower], 0)
    row = lax.broadcasted_iota(jnp.int32, (tile, n), 0)
    lane = lax.broadcasted_iota(jnp.int32, (tile, n), 1)
    mat = [gram[tile * r : tile * (r + 1), :] for r in range(blocks)]
    out = [jnp.where(lane == row + tile * r, 1.0, 0.0).astype(F32) for r in range(blocks)]
    for b in range(blocks):
        live = range(b, blocks)
        col = [
            {r: jnp.broadcast_to(mat[r][:, tile * b + s : tile * b + s + 1], (tile, n)) for r in live}
            for s in range(tile)
        ]
        inv = []
        for s in range(tile):
            inv.append(lax.rsqrt(col[s][b][s : s + 1, :]))
            for r in live:
                col[s][r] = col[s][r] * inv[s]
            for t in range(s + 1, tile):
                factor = col[s][b][t : t + 1, :]
                for r in live:
                    col[t][r] = col[t][r] - col[s][r] * factor
        top, left = mat[b], out[b]
        tops, lefts = [], []
        for s in range(tile):
            tops.append(top[s : s + 1, :] * inv[s])
            lefts.append(left[s : s + 1, :] * inv[s])
            if s + 1 < tile:
                low = jnp.where(row > s, col[s][b], 0.0)
                top = top - low * tops[s]
                left = left - low * lefts[s]
        inverse_ref[tile * b : tile * (b + 1), :] = jnp.concatenate(lefts, 0)
        for r in range(b + 1, blocks):
            for s in range(tile):
                mat[r] = mat[r] - col[s][r] * tops[s]
                out[r] = out[r] - col[s][r] * lefts[s]
    turned_ref[...] = inverse_ref[...].T * scale


def factor_inverse(mine, other, scale):
    rank = mine.shape[1]
    out = jax.ShapeDtypeStruct((rank, rank), F32)
    return pl.pallas_call(
        functools.partial(factor_body, scale=scale),
        out_shape=(out, out),
        in_specs=[WHOLE, WHOLE],
        out_specs=(WHOLE, WHOLE),
        compiler_params=PARAMS,
        cost_estimate=SLOW,
        name="factor",
    )(mine, other)


def basis_body(own_ref, turned_ref, basis_ref):
    basis_ref[...] = jnp.dot(
        own_ref[...], turned_ref[...], precision=lax.Precision.HIGHEST, preferred_element_type=F32
    )


def basis_of(own, turned):
    rows, rank = own.shape
    block = rows // 4
    return pl.pallas_call(
        basis_body,
        out_shape=jax.ShapeDtypeStruct((rows, rank), F32),
        grid=(rows // block,),
        in_specs=[
            pl.BlockSpec((block, rank), lambda i: (i, 0)),
            pl.BlockSpec((rank, rank), lambda i: (0, 0)),
        ],
        out_specs=pl.BlockSpec((block, rank), lambda i: (i, 0)),
        compiler_params=PARAMS,
        cost_estimate=COST,
        name="basis",
    )(own, turned)


def weigh_body(*refs, plan, block, width):
    total = None
    for turned, part, chunk, chunk_part in plan:
        size = refs[turned].shape[2]
        for at in range(0, size, block):
            rows = jnp.concatenate(split(refs[turned][part, :, at : at + block]), 0)
            here = slice(chunk_part * size + at, chunk_part * size + at + block)
            high, low = split(jnp.concatenate([refs[chunk][here, :], refs[chunk + 1][here, :]], 1))
            both = mm(rows, low) + mm(rows, high)
            total = both if total is None else total + both
    rank = total.shape[0] // 2
    total = total[rank:] + total[:rank]
    extra = refs[width:]
    if len(extra) > 1:
        total = extra[0][...] + total
    if len(extra) < 3:
        extra[-1][...] = total
        return
    total = jnp.dot(
        extra[1][...], total, precision=lax.Precision.HIGHEST, preferred_element_type=F32
    )
    first = lax.axis_index("core") == 0
    cols = rank
    keep, give = total[:, :cols], total[:, cols:]
    low_core = jnp.where(first, keep, give)
    high_core = jnp.where(first, give, keep)
    out_ref = extra[2]
    for part in range(out_ref.shape[0]):
        span = slice(part * (rank // 16), (part + 1) * (rank // 16))
        out_ref[part, 0] = low_core[span]
        out_ref[part, 1] = high_core[span]


def weigh(turned, chunks, plan, acc=None, inverse=None, block=384):
    rank = turned[0].shape[1]
    cols = chunks[0][0].shape[1]
    args = list(turned) + [array for chunk in chunks for array in chunk]
    width = len(args)
    args += [array for array in (acc, inverse) if array is not None]
    plan = [(t, part, len(turned) + 2 * c, chunk_part) for t, part, c, chunk_part in plan]
    if inverse is None:
        out = pltpu.VMEM((rank, 2 * cols), F32)
    else:
        out = jax.ShapeDtypeStruct((16, 2, rank // 16, cols), F32)
    return pl.pallas_call(
        functools.partial(weigh_body, plan=plan, block=block, width=width),
        out_shape=out,
        in_specs=[WHOLE] * len(args),
        out_specs=WHOLE,
        compiler_params=PARAMS,
        cost_estimate=COST,
        name="weigh",
    )(*args)


def total_body(parts_ref, out_ref):
    rows = out_ref.shape[0]
    total = parts_ref[:rows, :]
    for at in range(rows, parts_ref.shape[0], rows):
        total = total + parts_ref[at : at + rows, :]
    out_ref[...] = total


def total_of(parts, rows):
    return pl.pallas_call(
        total_body,
        out_shape=jax.ShapeDtypeStruct((rows, parts.shape[1]), F32),
        in_specs=[WHOLE],
        out_specs=WHOLE,
        compiler_params=PARAMS,
        cost_estimate=COST,
        name="total",
    )(parts)


def shards(panel, test_matrix, prior_sketch):
    rows, rank = prior_sketch.shape
    half = rows // 2
    total_rows = panel.shape[0] * lax.axis_size("y") * lax.axis_size("z")

    panel = pltpu.with_memory_space_constraint(panel, pltpu.HBM)
    test_other = swap(test_matrix)
    (far_give,) = fetch(panel, rows, (2, 1))
    panel, far_give, test_other = lax.optimization_barrier((panel, far_give, test_other))
    tests = (test_matrix, test_other)
    far_other = swap(far_give)
    far_keep, right_keep, left_keep, here_keep, *give = fetch(
        panel, rows, (2, 0), (1, 0), (3, 0), (0, 0), (1, 1), (3, 1), (0, 1)
    )
    far = (far_keep, far_other)
    far_top = term(far, 0, half, tests)
    far_bot = term(far, half, half, tests)
    far_top, far_bot, *give = lax.optimization_barrier((far_top, far_bot, *give))
    far_top = shift(far_top, "x", 1)
    far_bot = shift(far_bot, "x", 3)
    right = (right_keep, swap(give[0]))
    left = (left_keep, swap(give[1]))
    near_bot = term(right, half, half, tests)
    near_top = term(left, 0, half, tests)
    near_bot, near_top = lax.optimization_barrier((near_bot, near_top))
    near_bot = shift(near_bot, "x", 1)
    near_top = shift(near_top, "x", 3)
    here = (here_keep, swap(give[2]))
    base = term(here, 0, rows, tests, (prior_sketch,), (near_top, near_bot), cost=FIRST)
    far_top, far_bot = lax.optimization_barrier((far_top, far_bot))
    both_top = shift(term(right, 0, half, tests, (far_top,)), "x", 1)
    both_bot = shift(term(left, half, half, tests, (far_bot,)), "x", 3)
    own, turned = finish(base, both_top, both_bot)

    from_left = shift(turned, "x", 1)
    from_right = shift(turned, "x", 3)
    keep, give = gather(gram_of(own, turned))
    gram = keep + swap(give)
    acc = weigh([turned], [here], [(0, 0, 0, 0), (0, 1, 0, 1)])
    gram, acc = lax.optimization_barrier((axis_sum(gram, "y"), acc))
    gram = axis_sum(gram, "z")
    across = [shift(gram, "x", by) for by in (2, 1, 3)]
    gram, from_left, from_right = lax.optimization_barrier((gram, from_left, from_right))
    far_bot = shift(from_left[1:], "x", 1)
    far_top = shift(from_right[:1], "x", 3)
    acc = weigh(
        [from_left, from_right],
        [left, right],
        [(source, part, source, part) for source in range(2) for part in range(2)],
        acc,
    )
    acc, across = lax.optimization_barrier((acc, across))
    gram = gram + across[0] + across[1] + across[2]
    inverse, scaled = factor_inverse(gram, swap(gram), float(total_rows) ** 0.5)
    basis = basis_of(own, scaled)

    far_top, far_bot, inverse = lax.optimization_barrier((far_top, far_bot, inverse))
    weights = weigh([far_top, far_bot], [far], [(0, 0, 0, 0), (1, 0, 0, 1)], acc, inverse)
    parts = lax.all_to_all(weights.reshape(2 * rank, -1), ("y", "z", "core"), 0, 0, tiled=True)
    return basis, total_of(parts, rank // 16)


def solution(mesh):
    fine = Mesh(mesh.devices.reshape(4, 4, 4, 2), AXES)
    return jax.shard_map(
        shards,
        mesh=fine,
        in_specs=(P(("y", "z"), ("x", "core")), P(("x", "core"), None), P(AXES, None)),
        out_specs=(P(AXES, None), P(("y", "z"), ("x", "core"))),
        check_vma=False,
    )
```

```python
import functools

import jax
import jax.numpy as jnp
from jax import lax
from jax.experimental import pallas as pl
from jax.experimental.pallas import tpu as pltpu
from jax.sharding import Mesh, PartitionSpec as P

AXES = ("y", "z", "x", "core")
F32 = jnp.float32
BF16 = jnp.bfloat16
LIMIT = 16 * 1024 * 1024
COST = pl.CostEstimate(flops=0, bytes_accessed=0, transcendentals=0)
FIRST = pl.CostEstimate(flops=3 * 10**8, bytes_accessed=0, transcendentals=0)
SLOW = pl.CostEstimate(flops=13 * 10**8, bytes_accessed=0, transcendentals=0)
PARAMS = pltpu.CompilerParams(vmem_limit_bytes=LIMIT)
WHOLE = pl.BlockSpec(memory_space=pltpu.VMEM)


def shift(block, axis, by):
    n = lax.axis_size(axis)
    return lax.ppermute(block, axis, [(i, (i + by) % n) for i in range(n)])


def swap(block):
    return shift(block, "core", 1)


def axis_sum(block, axis):
    far, right, left = (shift(block, axis, by) for by in (2, 1, 3))
    return block + right + left + far


def split(block):
    high = block.astype(BF16)
    return high, (block - high.astype(F32)).astype(BF16)


def mm(a, b):
    return jnp.dot(a, b, preferred_element_type=F32)


def fetch_body(panel_ref, *rest, plan):
    outs, sems = rest[: len(plan)], rest[len(plan)]
    rows = outs[0].shape[0]
    x = lax.axis_index("x")
    core = lax.axis_index("core")
    copies = []
    for slot, (step, other) in enumerate(plan):
        chunk = lax.rem(x + step, 4) * 2 + (1 - core if other else core)
        start = pl.multiple_of(chunk * rows, rows)
        copies.append(
            pltpu.make_async_copy(panel_ref.at[pl.ds(start, rows), :], outs[slot], sems.at[slot])
        )
    for copy in copies:
        copy.start()
    for copy in copies:
        copy.wait()


def fetch(panel, rows, *plan):
    count = len(plan)
    cols = panel.shape[1]
    return pl.pallas_call(
        functools.partial(fetch_body, plan=plan),
        out_shape=[pltpu.VMEM((rows, cols), F32)] * count,
        in_specs=[pl.BlockSpec(memory_space=pl.ANY)],
        out_specs=[WHOLE] * count,
        scratch_shapes=[pltpu.SemaphoreType.DMA((count,))],
        compiler_params=PARAMS,
        cost_estimate=COST,
        name="fetch",
    )(panel)


def term_body(mine_ref, other_ref, test_ref, test_other_ref, *rest, first, sizes, block):
    rank = test_ref.shape[1]
    tests = jnp.concatenate([test_ref[...], test_other_ref[...]], 0)
    tests = jnp.concatenate(split(tests), 1)
    out_ref = rest[-1]
    for at in range(0, out_ref.shape[0], block):
        here = slice(first + at, first + at + block)
        high, low = split(jnp.concatenate([mine_ref[here, :], other_ref[here, :]], 1))
        both = mm(low, tests) + mm(high, tests)
        total = both[:, rank:] + both[:, :rank]
        slot = 0
        for size in sizes:
            addend_ref = rest[slot + at // (out_ref.shape[0] // size)]
            begin = at % (out_ref.shape[0] // size)
            total = total + addend_ref[begin : begin + block, :]
            slot += size
        out_ref[at : at + block, :] = total


def term(chunk, first, count, tests, *addends, block=384, cost=COST):
    rank = tests[0].shape[1]
    sizes = tuple(len(parts) for parts in addends)
    return pl.pallas_call(
        functools.partial(term_body, first=first, sizes=sizes, block=block),
        out_shape=pltpu.VMEM((count, rank), F32),
        in_specs=[WHOLE] * (4 + sum(sizes)),
        out_specs=WHOLE,
        compiler_params=PARAMS,
        cost_estimate=cost,
        name="term",
    )(*chunk, *tests, *(array for parts in addends for array in parts))


def finish_body(base_ref, top_ref, bot_ref, own_ref, turned_ref):
    parts, _, size = turned_ref.shape
    for part in range(parts):
        span = slice(part * size, (part + 1) * size)
        both_ref = top_ref if part < parts // 2 else bot_ref
        begin = part % (parts // 2) * size
        own = base_ref[span, :] + both_ref[begin : begin + size, :]
        own_ref[span, :] = own
        turned_ref[part] = own.T


def finish(base, top, bot, parts=2):
    rows, rank = base.shape
    return pl.pallas_call(
        finish_body,
        out_shape=(
            pltpu.VMEM((rows, rank), F32),
            pltpu.VMEM((parts, rank, rows // parts), F32),
        ),
        in_specs=[WHOLE] * 3,
        out_specs=(WHOLE, WHOLE),
        compiler_params=PARAMS,
        cost_estimate=COST,
        name="finish",
    )(base, top, bot)


def gram_body(own_ref, turned_ref, gram_ref):
    parts, _, size = turned_ref.shape
    dot = functools.partial(jnp.dot, precision=lax.Precision.HIGHEST, preferred_element_type=F32)
    total = None
    for part in range(parts):
        piece = dot(turned_ref[part], own_ref[part * size : (part + 1) * size, :])
        total = piece if total is None else total + piece
    gram_ref[...] = total


def gram_of(own, turned):
    rank = own.shape[1]
    return pl.pallas_call(
        gram_body,
        out_shape=pltpu.VMEM((rank, rank), F32),
        in_specs=[WHOLE] * 2,
        out_specs=WHOLE,
        compiler_params=PARAMS,
        cost_estimate=COST,
        name="gram",
    )(own, turned)


def gather_body(*refs):
    keep_ref, give_ref = refs[-2:]
    half = keep_ref.shape[0]
    core = lax.axis_index("core")
    for out_ref, part in ((keep_ref, core), (give_ref, 1 - core)):
        here = pl.ds(pl.multiple_of(part * half, half), half)
        total = refs[0][here, :]
        for ref in refs[1:-2]:
            total = total + ref[here, :]
        out_ref[...] = total


def gather(*parts):
    rank = parts[0].shape[1]
    return pl.pallas_call(
        gather_body,
        out_shape=(pltpu.VMEM((rank // 2, rank), F32),) * 2,
        in_specs=[WHOLE] * len(parts),
        out_specs=(WHOLE, WHOLE),
        compiler_params=PARAMS,
        cost_estimate=COST,
        name="gather",
    )(*parts)


def factor_body(mine_ref, other_ref, inverse_ref, turned_ref, *, scale, tile=8):
    half, n = mine_ref.shape
    blocks = n // tile
    first = lax.axis_index("core") == 0
    upper = jnp.where(first, mine_ref[...], other_ref[...])
    lower = jnp.where(first, other_ref[...], mine_ref[...])
    gram = jnp.concatenate([upper, lower], 0)
    row = lax.broadcasted_iota(jnp.int32, (tile, n), 0)
    lane = lax.broadcasted_iota(jnp.int32, (tile, n), 1)
    mat = [gram[tile * r : tile * (r + 1), :] for r in range(blocks)]
    out = [jnp.where(lane == row + tile * r, 1.0, 0.0).astype(F32) for r in range(blocks)]
    for b in range(blocks):
        live = range(b, blocks)
        col = [
            {r: jnp.broadcast_to(mat[r][:, tile * b + s : tile * b + s + 1], (tile, n)) for r in live}
            for s in range(tile)
        ]
        inv = []
        for s in range(tile):
            inv.append(lax.rsqrt(col[s][b][s : s + 1, :]))
            for r in live:
                col[s][r] = col[s][r] * inv[s]
            for t in range(s + 1, tile):
                factor = col[s][b][t : t + 1, :]
                for r in live:
                    col[t][r] = col[t][r] - col[s][r] * factor
        top, left = mat[b], out[b]
        tops, lefts = [], []
        for s in range(tile):
            tops.append(top[s : s + 1, :] * inv[s])
            lefts.append(left[s : s + 1, :] * inv[s])
            if s + 1 < tile:
                low = jnp.where(row > s, col[s][b], 0.0)
                top = top - low * tops[s]
                left = left - low * lefts[s]
        inverse_ref[tile * b : tile * (b + 1), :] = jnp.concatenate(lefts, 0)
        for r in range(b + 1, blocks):
            for s in range(tile):
                mat[r] = mat[r] - col[s][r] * tops[s]
                out[r] = out[r] - col[s][r] * lefts[s]
    turned_ref[...] = inverse_ref[...].T * scale


def factor_inverse(mine, other, scale):
    rank = mine.shape[1]
    out = jax.ShapeDtypeStruct((rank, rank), F32)
    return pl.pallas_call(
        functools.partial(factor_body, scale=scale),
        out_shape=(out, out),
        in_specs=[WHOLE, WHOLE],
        out_specs=(WHOLE, WHOLE),
        compiler_params=PARAMS,
        cost_estimate=SLOW,
        name="factor",
    )(mine, other)


def basis_body(own_ref, turned_ref, basis_ref):
    basis_ref[...] = jnp.dot(
        own_ref[...], turned_ref[...], precision=lax.Precision.HIGHEST, preferred_element_type=F32
    )


def basis_of(own, turned):
    rows, rank = own.shape
    block = rows // 4
    return pl.pallas_call(
        basis_body,
        out_shape=jax.ShapeDtypeStruct((rows, rank), F32),
        grid=(rows // block,),
        in_specs=[
            pl.BlockSpec((block, rank), lambda i: (i, 0)),
            pl.BlockSpec((rank, rank), lambda i: (0, 0)),
        ],
        out_specs=pl.BlockSpec((block, rank), lambda i: (i, 0)),
        compiler_params=PARAMS,
        cost_estimate=COST,
        name="basis",
    )(own, turned)


def weigh_body(*refs, plan, block, width):
    total = None
    for turned, part, chunk, chunk_part in plan:
        size = refs[turned].shape[2]
        for at in range(0, size, block):
            rows = jnp.concatenate(split(refs[turned][part, :, at : at + block]), 0)
            here = slice(chunk_part * size + at, chunk_part * size + at + block)
            high, low = split(jnp.concatenate([refs[chunk][here, :], refs[chunk + 1][here, :]], 1))
            both = mm(rows, low) + mm(rows, high)
            total = both if total is None else total + both
    rank = total.shape[0] // 2
    total = total[rank:] + total[:rank]
    extra = refs[width:]
    if len(extra) > 1:
        total = extra[0][...] + total
    if len(extra) < 3:
        extra[-1][...] = total
        return
    total = jnp.dot(
        extra[1][...], total, precision=lax.Precision.HIGHEST, preferred_element_type=F32
    )
    first = lax.axis_index("core") == 0
    cols = rank
    keep, give = total[:, :cols], total[:, cols:]
    low_core = jnp.where(first, keep, give)
    high_core = jnp.where(first, give, keep)
    out_ref = extra[2]
    for part in range(out_ref.shape[0]):
        span = slice(part * (rank // 16), (part + 1) * (rank // 16))
        out_ref[part, 0] = low_core[span]
        out_ref[part, 1] = high_core[span]


def weigh(turned, chunks, plan, acc=None, inverse=None, block=384):
    rank = turned[0].shape[1]
    cols = chunks[0][0].shape[1]
    args = list(turned) + [array for chunk in chunks for array in chunk]
    width = len(args)
    args += [array for array in (acc, inverse) if array is not None]
    plan = [(t, part, len(turned) + 2 * c, chunk_part) for t, part, c, chunk_part in plan]
    if inverse is None:
        out = pltpu.VMEM((rank, 2 * cols), F32)
    else:
        out = jax.ShapeDtypeStruct((16, 2, rank // 16, cols), F32)
    return pl.pallas_call(
        functools.partial(weigh_body, plan=plan, block=block, width=width),
        out_shape=out,
        in_specs=[WHOLE] * len(args),
        out_specs=WHOLE,
        compiler_params=PARAMS,
        cost_estimate=COST,
        name="weigh",
    )(*args)


def total_body(parts_ref, out_ref):
    rows = out_ref.shape[0]
    total = parts_ref[:rows, :]
    for at in range(rows, parts_ref.shape[0], rows):
        total = total + parts_ref[at : at + rows, :]
    out_ref[...] = total


def total_of(parts, rows):
    return pl.pallas_call(
        total_body,
        out_shape=jax.ShapeDtypeStruct((rows, parts.shape[1]), F32),
        in_specs=[WHOLE],
        out_specs=WHOLE,
        compiler_params=PARAMS,
        cost_estimate=COST,
        name="total",
    )(parts)


def shards(panel, test_matrix, prior_sketch):
    rows, rank = prior_sketch.shape
    half = rows // 2
    total_rows = panel.shape[0] * lax.axis_size("y") * lax.axis_size("z")

    panel = pltpu.with_memory_space_constraint(panel, pltpu.HBM)
    test_other = swap(test_matrix)
    (far_give,) = fetch(panel, rows, (2, 1))
    panel, far_give, test_other = lax.optimization_barrier((panel, far_give, test_other))
    tests = (test_matrix, test_other)
    far_other = swap(far_give)
    far_keep, right_keep, left_keep, here_keep, *give = fetch(
        panel, rows, (2, 0), (1, 0), (3, 0), (0, 0), (1, 1), (3, 1), (0, 1)
    )
    far = (far_keep, far_other)
    far_top = term(far, 0, half, tests)
    far_bot = term(far, half, half, tests)
    far_top, far_bot, *give = lax.optimization_barrier((far_top, far_bot, *give))
    far_top = shift(far_top, "x", 1)
    far_bot = shift(far_bot, "x", 3)
    right = (right_keep, swap(give[0]))
    left = (left_keep, swap(give[1]))
    near_bot = term(right, half, half, tests)
    near_top = term(left, 0, half, tests)
    near_bot, near_top = lax.optimization_barrier((near_bot, near_top))
    near_bot = shift(near_bot, "x", 1)
    near_top = shift(near_top, "x", 3)
    here = (here_keep, swap(give[2]))
    base = term(here, 0, rows, tests, (prior_sketch,), (near_top, near_bot), cost=FIRST)
    far_top, far_bot = lax.optimization_barrier((far_top, far_bot))
    both_top = shift(term(right, 0, half, tests, (far_top,)), "x", 1)
    both_bot = shift(term(left, half, half, tests, (far_bot,)), "x", 3)
    own, turned = finish(base, both_top, both_bot)

    from_right = shift(turned, "x", 3)
    keep, give = gather(gram_of(own, turned))
    keep, give, turned = lax.optimization_barrier((keep, give, turned))
    from_left = shift(turned, "x", 1)
    gram = keep + swap(give)
    gram = axis_sum(axis_sum(gram, "y"), "z")
    across = [shift(gram, "x", by) for by in (2, 1, 3)]
    gram, from_left, from_right, turned = lax.optimization_barrier(
        (gram, from_left, from_right, turned)
    )
    far_bot = shift(from_left[1:], "x", 1)
    far_top = shift(from_right[:1], "x", 3)
    acc = weigh(
        [turned, from_left, from_right],
        [here, left, right],
        [(source, part, source, part) for source in range(3) for part in range(2)],
    )
    acc, across = lax.optimization_barrier((acc, across))
    gram = gram + across[0] + across[1] + across[2]
    inverse, scaled = factor_inverse(gram, swap(gram), float(total_rows) ** 0.5)
    basis = basis_of(own, scaled)

    far_top, far_bot, inverse = lax.optimization_barrier((far_top, far_bot, inverse))
    weights = weigh([far_top, far_bot], [far], [(0, 0, 0, 0), (1, 0, 0, 1)], acc, inverse)
    parts = lax.all_to_all(weights.reshape(2 * rank, -1), ("y", "z", "core"), 0, 0, tiled=True)
    return basis, total_of(parts, rank // 16)


def solution(mesh):
    fine = Mesh(mesh.devices.reshape(4, 4, 4, 2), AXES)
    return jax.shard_map(
        shards,
        mesh=fine,
        in_specs=(P(("y", "z"), ("x", "core")), P(("x", "core"), None), P(AXES, None)),
        out_specs=(P(AXES, None), P(("y", "z"), ("x", "core"))),
        check_vma=False,
    )
```
